32 devices in a mesh: groups: 2 (over y), expert: 4 (over z), dp: 2 (over x), inner: 2 (over core).
Axes of the slice: x: 2, y: 2, z: 4, core: 2. Of those that a mesh axis runs over, the one named last changes fastest.
Arguments:
- tokens: bfloat16 [2048, 2048], P(('groups', 'expert', 'inner'), 'dp'), parts along dimension 0, may hold values from -6 to 6
- out_grad: bfloat16 [2048, 2048], P(('groups', 'expert', 'inner'), 'dp'), parts along dimension 0, may hold values from -2.5 to 2.5
- expert_ids: int32 [2048, 2], P(('groups', 'expert', 'inner')), parts along dimension 0, may hold values from 0 to 7, all different within a row; in each aligned block of 128 rows (0 to 127, 128 to 255, ...) at most 48 rows name the same one
- gate_weights: float32 [2048, 2], P(('groups', 'expert', 'inner')), parts along dimension 0, may hold values from 0.2 to 1
- shadow_expert: int32 [4], replicated, may hold values from 0 to 7, as said below
- w_gate: bfloat16 [8, 2048, 1024], P('expert', 'dp', 'inner'), may hold values from -0.125 to 0.125
- w_up: bfloat16 [8, 2048, 1024], P('expert', 'dp', 'inner'), may hold values from -0.125 to 0.125
- w_down: bfloat16 [8, 1024, 2048], P('expert', 'inner', 'dp'), may hold values from -0.1875 to 0.1875
- copy_gate: bfloat16 [4, 2048, 1024], P('expert', 'dp', 'inner'), may hold values from -0.125 to 0.125
- copy_up: bfloat16 [4, 2048, 1024], P('expert', 'dp', 'inner'), may hold values from -0.125 to 0.125
- copy_down: bfloat16 [4, 1024, 2048], P('expert', 'inner', 'dp'), may hold values from -0.1875 to 0.1875
Outputs:
- grad_tokens: bfloat16 [2048, 2048], P(('groups', 'expert', 'inner'), 'dp'), parts along dimension 0
- grad_w_gate: bfloat16 [16, 2048, 1024], P(('groups', 'expert'), 'dp', 'inner'), parts along dimension 0
- grad_w_up: bfloat16 [16, 2048, 1024], P(('groups', 'expert'), 'dp', 'inner'), parts along dimension 0
- grad_w_down: bfloat16 [16, 1024, 2048], P(('groups', 'expert'), 'inner', 'dp'), parts along dimension 0
The draws below stay inside these ranges and needn't reach their ends.
There are 2 independent parts, one for each index of `groups`. The reference program is written for one: setup_inputs(seed, part) draws one part's arguments, and reference() takes and returns one part's arrays. A program takes and returns all parts, laid end to end along the dimension named above; an argument that names none is the same for every part. Nothing has to cross between parts.
Inputs may be any that keep to these rules, and one draw needn't show every extreme that they name: `expert_ids`: A token's two experts differ; among the 128 tokens of one index of expert+inner no expert is named more than 48 times, a bound that some block reaches. Experts 2 j and 2 j + 1 are owned by index j of expert. `shadow_expert`: entry j names an expert that index j does not own. Exactly half of the indices of expert own the experts of two entries each, the other indices those of none; the two entries that fall on one index may name the same expert or its two experts.
All inputs are finite; a program needn't handle non-finite values.
Results may differ from the reference program's by a relative error of at most 0.02.
Values may be sent and summed in bfloat16 or wider, within the bound.
No kernel may reach another device: no remote copies, remote signals or barrier semaphores. Data moves between devices by JAX's collectives and lax.ppermute only.
A program may use at most 128 MiB of HBM per device.

```python
import math
import jax
import jax.numpy as jnp
import numpy as np
from jax import lax

D = 2048
H = 1024
TOK_DEV = 128
TOKENS = 1024
EXPERTS = 8
MOST = 48
N_EXPERT = 4
N_DP = 2


def draw_shadow_expert(key, part):
    first_key, second_key = jax.random.split(jax.random.fold_in(key, 17))
    order = jax.random.permutation(first_key, N_EXPERT).astype(jnp.int32)
    position = jnp.arange(N_EXPERT, dtype=jnp.int32)
    owner_by_position = order[(2 * (position // 2) + 2) % N_EXPERT]
    target = jnp.zeros((N_EXPERT,), jnp.int32).at[order].set(owner_by_position)
    member_bit = jax.random.randint(second_key, (N_EXPERT,), 0, 2)
    return (2 * target + member_bit).astype(jnp.int32)


def block_levels(rng, shape, cuts, least, largest):
    def one(dim, parts):
        draws = jax.random.uniform(jax.random.fold_in(jax.random.fold_in(rng, 6), dim), (parts,), jnp.float32, least / len(cuts), largest / len(cuts))
        return jnp.repeat(jnp.exp(draws), shape[dim] // parts).reshape((-1,) + (1,) * (len(shape) - dim - 1))

    factor_of = one(*cuts[0])
    for cut in cuts[1:]:
        factor_of = factor_of * one(*cut)
    return factor_of


def assign_block(key, own, number, rows, count, top, most, skew):
    ranking = jax.random.permutation(key, count)
    heavy_load, usual = portions_of(count, rows * top, most, skew, True), portions_of(count, rows * top, most, skew, False)
    places = jnp.arange(count)

    def named(tallies, turn):
        used = int((tallies > 0).sum())
        fixed = max(1, used // 4)
        moved = fixed + (places - fixed + turn * (used - fixed)) % max(1, count - fixed)
        return jnp.zeros((count,), jnp.int32).at[ranking[jnp.where(places < fixed, places, moved)]].set(jnp.asarray(tallies, jnp.int32))

    tallies = jnp.where(number % 4 == 0, named(heavy_load, number // 4), named(usual, number - number // 4 - 1))
    mixed = jax.random.permutation(jax.random.fold_in(own, 3), count)
    source_of, taker = mixed[0:count // 2 * 2:2], mixed[1:count // 2 * 2:2]
    room = jnp.minimum(tallies[source_of] - 1, most - tallies[taker]) // 2
    room = jnp.where((source_of == ranking[0]) | (taker == ranking[0]) | (tallies[taker] == 0), 0, jnp.maximum(room, 0))
    moved = jax.random.randint(jax.random.fold_in(own, 4), (count // 2,), 0, 1 << 20) % (room + 1)
    tallies = tallies.at[source_of].add(-moved).at[taker].add(moved)
    items = jnp.searchsorted(jnp.cumsum(tallies), jnp.arange(rows * top), side="right").astype(jnp.int32)
    table = items.reshape(top, rows).T
    table = table[jax.random.permutation(jax.random.fold_in(own, 1), rows)]
    turn = jax.random.randint(jax.random.fold_in(own, 2), (rows, 1), 0, top)
    return jnp.take_along_axis(table, (jnp.arange(top)[None, :] + turn) % top, axis=1)


def portions_of(amount, total, bound, lean, full):
    weights = [(1 << 20) // math.isqrt(standing ** lean) + 1 for standing in range(1, amount + 1)]
    largest = bound if full else min(bound, max(-(-total // amount), total * weights[0] // sum(weights)))
    least = 1 if total - largest >= amount - 1 else 0
    given, surplus = [largest] + [least] * (amount - 1), total - largest - least * (amount - 1)
    while surplus > 0:
        candidates = [i for i in range(1, amount) if given[i] < largest] or [i for i in range(1, amount) if given[i] < bound]
        mass, budget = sum([weights[i] for i in candidates]), surplus
        for i in candidates:
            extra = min(bound - given[i], max(1, budget * weights[i] // mass), surplus)
            given[i] = given[i] + extra
            surplus = surplus - extra
    return np.array(given)


def noise(key, shape, spread, limit, shards=(), held_as=jnp.bfloat16):
    array = jax.random.normal(key, shape, jnp.float32) * spread
    if len(shards) > 0:
        array = block_levels(key, shape, shards, -0.22, 0.18) * array
    return jnp.clip(array, min=-limit, max=limit).astype(held_as)


def setup_inputs(seed: int = 0, part: int = 0) -> dict:
    arg_keys = jax.random.split(jax.random.key(seed), 12)
    own_keys = jax.random.split(jax.random.fold_in(arg_keys[11], part), 12)
    tokens = noise(own_keys[0], (TOKENS, D), 1.0, 6.0, ((0, 8), (1, 2)))
    out_grad = noise(own_keys[1], (TOKENS, D), 0.3, 2.5, ((0, 8), (1, 2)))
    expert_ids_keys = jax.random.split(jax.random.fold_in(own_keys[2], 1), TOKENS // TOK_DEV)
    expert_ids_turns = jax.random.permutation(jax.random.fold_in(own_keys[2], 3), TOKENS // TOK_DEV)
    expert_ids = jax.vmap(lambda own, number: assign_block(jax.random.fold_in(own_keys[2], 2), own, number, TOK_DEV, EXPERTS, 2, MOST, 2))(expert_ids_keys, expert_ids_turns).reshape((TOKENS, 2))
    gate_weights = jnp.clip(0.2 + 0.8 * jax.random.uniform(own_keys[3], (TOKENS, 2), jnp.float32) ** block_levels(own_keys[3], (TOKENS, 2), ((0, 8),), -0.2, 0.2), 0.2, 1.0)
    shadow_expert = draw_shadow_expert(jax.random.fold_in(arg_keys[11], 71), part)
    w_gate = noise(arg_keys[5], (EXPERTS, D, H), D ** -0.5, 0.125, ((0, 4), (1, 2), (2, 2)))
    w_up = noise(arg_keys[6], (EXPERTS, D, H), D ** -0.5, 0.125, ((0, 4), (1, 2), (2, 2)))
    w_down = noise(arg_keys[7], (EXPERTS, H, D), H ** -0.5, 0.1875, ((0, 4), (1, 2), (2, 2)))
    copy_gate = noise(arg_keys[8], (N_EXPERT, D, H), D ** -0.5, 0.125, ((0, 4), (1, 2), (2, 2)))
    copy_up = noise(arg_keys[9], (N_EXPERT, D, H), D ** -0.5, 0.125, ((0, 4), (1, 2), (2, 2)))
    copy_down = noise(arg_keys[10], (N_EXPERT, H, D), H ** -0.5, 0.1875, ((0, 4), (1, 2), (2, 2)))
    return {"tokens": tokens, "out_grad": out_grad, "expert_ids": expert_ids, "gate_weights": gate_weights, "shadow_expert": shadow_expert, "w_gate": w_gate, "w_up": w_up, "w_down": w_down, "copy_gate": copy_gate, "copy_up": copy_up, "copy_down": copy_down}


def serving_copy(expert_ids, shadow_expert, first_token):
    tok_rows = expert_ids.shape[0]
    shadow_count = shadow_expert.shape[0]
    token_index = first_token + jnp.arange(tok_rows, dtype=jnp.int32)
    position = token_index[:, None] + jnp.arange(2, dtype=jnp.int32)[None, :]
    matches = (expert_ids[:, :, None] == shadow_expert[None, None, :]).astype(jnp.int32)
    copies = 1 + jnp.sum(matches, axis=2)
    chosen = position % copies
    slot_order = jnp.arange(shadow_count, dtype=jnp.int32)
    lower_slot = (slot_order[:, None] > slot_order[None, :]).astype(jnp.int32)
    same_expert = (shadow_expert[:, None] == shadow_expert[None, :]).astype(jnp.int32)
    rank_among = jnp.sum(lower_slot * same_expert, axis=1)
    picked = matches * (rank_among[None, None, :] == chosen[:, :, None] - 1).astype(jnp.int32)
    holder = jnp.sum(picked * slot_order[None, None, :], axis=2)
    shadowed = jnp.sum(picked, axis=2)
    return jnp.where(shadowed > 0, 2 * shadow_count + holder, expert_ids).astype(jnp.int32)


def activation(block_sums):
    width_half = block_sums.shape[-1] // 3
    pre_gate = block_sums[..., :width_half]
    pre_up = block_sums[..., width_half:2 * width_half]
    hidden_grad = block_sums[..., 2 * width_half:]
    sigmoid_gate = jax.nn.sigmoid(pre_gate)
    swish_gate = pre_gate * sigmoid_gate
    grad_up = (hidden_grad * swish_gate).astype(jnp.bfloat16)
    grad_gate = (hidden_grad * pre_up * sigmoid_gate * (1.0 + pre_gate * (1.0 - sigmoid_gate))).astype(jnp.bfloat16)
    hidden = (swish_gate * pre_up).astype(jnp.bfloat16)
    return grad_gate, grad_up, hidden


def settle(partial_blocks):
    rounded = lax.optimization_barrier(partial_blocks.astype(jnp.bfloat16))
    return jnp.sum(rounded.astype(jnp.float32), axis=1)


def copy_backward(inputs, grad_rows, weight_gate, weight_up, weight_down):
    row_count = inputs.shape[0]
    slice_width = D // N_DP
    split_in = inputs.astype(jnp.float32).reshape(row_count, N_DP, slice_width)
    split_grad = grad_rows.astype(jnp.float32).reshape(row_count, N_DP, slice_width)
    gate_blocks = weight_gate.astype(jnp.float32).reshape(N_DP, slice_width, H)
    up_blocks = weight_up.astype(jnp.float32).reshape(N_DP, slice_width, H)
    down_blocks = weight_down.astype(jnp.float32).reshape(H, N_DP, slice_width)
    pre_sums = jnp.concatenate([
        settle(jnp.einsum("rps,psh->rph", split_in, gate_blocks)),
        settle(jnp.einsum("rps,psh->rph", split_in, up_blocks)),
        settle(jnp.einsum("rps,hps->rph", split_grad, down_blocks))], axis=1)
    grad_gate, grad_up, hidden = activation(pre_sums)
    gate_wide = grad_gate.astype(jnp.float32)
    up_wide = grad_up.astype(jnp.float32)
    route_grad = jnp.einsum("rh,dh->rd", gate_wide, weight_gate.astype(jnp.float32)) + jnp.einsum("rh,dh->rd", up_wide, weight_up.astype(jnp.float32))
    inputs_wide = inputs.astype(jnp.float32)
    dw_gate = jnp.einsum("rd,rh->dh", inputs_wide, gate_wide)
    dw_up = jnp.einsum("rd,rh->dh", inputs_wide, up_wide)
    dw_down = jnp.einsum("rh,rd->hd", hidden.astype(jnp.float32), grad_rows.astype(jnp.float32))
    return route_grad, dw_gate, dw_up, dw_down


def reference(tokens, out_grad, expert_ids, gate_weights, shadow_expert, w_gate, w_up, w_down, copy_gate, copy_up, copy_down):
    copy_ids = serving_copy(expert_ids, shadow_expert, jnp.int32(0))
    flat_ids = copy_ids.reshape(-1)
    flat_gates = gate_weights.reshape(-1).astype(jnp.float32)
    capacity = (TOKENS // TOK_DEV) * MOST

    def gather_rows(copy_number):
        served = flat_ids == copy_number
        served_count = jnp.sum(served.astype(jnp.int32))
        route_index = jnp.nonzero(served, size=capacity, fill_value=0)[0].astype(jnp.int32)
        valid_route = (jnp.arange(capacity, dtype=jnp.int32) < served_count).astype(jnp.float32)
        token_row = route_index // 2
        inputs = tokens[token_row]
        grad_rows = ((flat_gates[route_index] * valid_route)[:, None] * out_grad[token_row].astype(jnp.float32)).astype(jnp.bfloat16)
        return token_row, inputs, grad_rows

    def shadow_step(dx_total, stacked):
        copy_number, weight_gate, weight_up, weight_down = stacked
        token_row, inputs, grad_rows = gather_rows(copy_number)
        route_grad, dw_gate, dw_up, dw_down = copy_backward(inputs, grad_rows, weight_gate, weight_up, weight_down)
        dx_total = dx_total.at[token_row].add(route_grad)
        return dx_total, (dw_gate.astype(jnp.bfloat16), dw_up.astype(jnp.bfloat16), dw_down.astype(jnp.bfloat16))

    dx_total = jnp.zeros((TOKENS, D), jnp.float32)
    shadow_numbers = EXPERTS + jnp.arange(N_EXPERT, dtype=jnp.int32)
    dx_total, panels = lax.scan(shadow_step, dx_total, (shadow_numbers, copy_gate, copy_up, copy_down))

    def owner_step(dx_total, stacked):
        copy_number, weight_gate, weight_up, weight_down = stacked
        token_row, inputs, grad_rows = gather_rows(copy_number)
        route_grad, dw_gate, dw_up, dw_down = copy_backward(inputs, grad_rows, weight_gate, weight_up, weight_down)
        dx_total = dx_total.at[token_row].add(route_grad)
        indicator = (shadow_expert == copy_number).astype(jnp.float32)
        gate_total = dw_gate + jnp.einsum("j,jdh->dh", indicator, panels[0].astype(jnp.float32))
        up_total = dw_up + jnp.einsum("j,jdh->dh", indicator, panels[1].astype(jnp.float32))
        down_total = dw_down + jnp.einsum("j,jhd->hd", indicator, panels[2].astype(jnp.float32))
        return dx_total, (gate_total.astype(jnp.bfloat16), up_total.astype(jnp.bfloat16), down_total.astype(jnp.bfloat16))

    owner_numbers = jnp.arange(EXPERTS, dtype=jnp.int32)
    dx_total, owned = lax.scan(owner_step, dx_total, (owner_numbers, w_gate, w_up, w_down))
    return (dx_total.astype(jnp.bfloat16), owned[0], owned[1], owned[2])
```

```python
import functools

import jax
import jax.numpy as jnp
from jax import lax
from jax.experimental import pallas as pl
from jax.experimental.pallas import tpu as pltpu
from jax.sharding import PartitionSpec as P

META = 16
VMEM_BYTES = 56 * 1024 * 1024


def call(body, out_shape, in_specs, out_specs, scratch, flops, moved, **kw):
    return pl.pallas_call(
        body,
        out_shape=out_shape,
        in_specs=in_specs,
        out_specs=out_specs,
        scratch_shapes=scratch,
        compiler_params=pltpu.CompilerParams(vmem_limit_bytes=VMEM_BYTES),
        cost_estimate=pl.CostEstimate(flops=flops, bytes_accessed=moved, transcendentals=0),
        **kw,
    )


WHOLE = pl.BlockSpec(memory_space=pltpu.VMEM)
SCALARS = pl.BlockSpec(memory_space=pltpu.SMEM)
REMAIN = pl.BlockSpec(memory_space=pl.ANY)


def pack_kernel(shadow_count, info, shadow, tok_ref, grad_ref, meta_ref, out_ref):
    rows = tok_ref.shape[0]
    out_ref[0:rows, :] = tok_ref[...]
    out_ref[rows : 2 * rows, :] = grad_ref[...]
    meta = meta_ref[...]
    ids, gates = meta[0:2], meta[2:4]
    choice = lax.broadcasted_iota(jnp.int32, ids.shape, 0)
    position = info[2] * rows + lax.broadcasted_iota(jnp.int32, ids.shape, 1) + choice
    position = position.astype(jnp.float32)
    entry = [shadow[j] for j in range(shadow_count)]
    named = [ids == e.astype(jnp.float32) for e in entry]
    copies = jnp.ones(ids.shape, jnp.float32)
    for hit in named:
        copies = copies + jnp.where(hit, 1.0, 0.0)
    halves = position - 2.0 * jnp.floor((position + 0.5) * 0.5)
    thirds = position - 3.0 * jnp.floor((position + 0.5) * (1.0 / 3.0))
    chosen = jnp.where(copies == 2.0, halves, jnp.where(copies == 3.0, thirds, 0.0))
    serving = ids
    for j in range(shadow_count):
        before = jnp.int32(0)
        for i in range(j):
            before = before + jnp.where(entry[i] == entry[j], 1, 0)
        take = named[j] & (chosen == (before + 1).astype(jnp.float32))
        serving = jnp.where(take, float(2 * shadow_count + j), serving)
    high = gates.astype(jnp.bfloat16)
    rest = gates - high.astype(jnp.float32)
    middle = rest.astype(jnp.bfloat16)
    low = (rest - middle.astype(jnp.float32)).astype(jnp.bfloat16)
    block = jnp.concatenate(
        [
            serving,
            high.astype(jnp.float32),
            middle.astype(jnp.float32),
            low.astype(jnp.float32),
            jnp.zeros((META - 8, rows), jnp.float32),
        ],
        axis=0,
    )
    out_ref[2 * rows : 2 * rows + META, :] = jnp.zeros((META, tok_ref.shape[1]), jnp.bfloat16)
    out_ref[2 * rows : 2 * rows + META, 0:rows] = block.astype(jnp.bfloat16)


def routing(own_ref, sib_ref, rows):
    meta = jnp.concatenate(
        [
            own_ref[2 * rows : 2 * rows + META, 0:rows].astype(jnp.float32),
            sib_ref[2 * rows : 2 * rows + META, 0:rows].astype(jnp.float32),
        ],
        axis=1,
    )
    return meta[0:1], meta[1:2], meta[2:3] + meta[4:5] + meta[6:7], meta[3:4] + meta[5:6] + meta[7:8]


def row_codes(meta, numbers):
    first, second, gate_a, gate_b = meta
    tokens = first.shape[1]
    hit_a, hit_b = first == numbers, second == numbers
    hit = jnp.where(hit_a | hit_b, 1.0, 0.0)
    gate = jnp.where(hit_a, gate_a, 0.0) + jnp.where(hit_b, gate_b, 0.0)
    earlier = lax.broadcasted_iota(jnp.int32, (tokens, tokens), 0) < lax.broadcasted_iota(
        jnp.int32, (tokens, tokens), 1
    )
    rank = jnp.dot(
        hit.astype(jnp.bfloat16),
        jnp.where(earlier, 1.0, 0.0).astype(jnp.bfloat16),
        preferred_element_type=jnp.float32,
    )
    return jnp.where(hit > 0.0, rank, -1.0), gate


def gather_rows(codes, gate, index, cap, tok, grad):
    tokens = codes.shape[1]
    place = lax.broadcasted_iota(jnp.int32, (cap, tokens), 0).astype(jnp.float32) == codes[
        index : index + 1, :
    ]
    row_gate = jnp.sum(jnp.where(place, gate[index : index + 1, :], 0.0), axis=1, keepdims=True)
    place = jnp.where(place, 1.0, 0.0).astype(jnp.bfloat16)
    inputs = jnp.dot(place, tok, preferred_element_type=jnp.float32).astype(jnp.bfloat16)
    grads = jnp.dot(place, grad, preferred_element_type=jnp.float32)
    return place, inputs, (grads * row_gate).astype(jnp.bfloat16)


def copy_numbers(z, shadow_count):
    slot = lax.broadcasted_iota(jnp.int32, (8, 1), 0)
    number = jnp.where(slot < 2, 2 * z + slot, jnp.where(slot == 2, 2 * shadow_count + z, -1))
    return number.astype(jnp.float32)


NT = (((1,), (1,)), ((), ()))
TN = (((0,), (0,)), ((), ()))


def fetch(pairs, sems):
    copies = []
    for i, (src, dst) in enumerate(pairs):
        copies.append(pltpu.make_async_copy(src, dst, sems.at[i]))
        copies[-1].start()
    return copies


def forward_kernel(shadow_count, cap, chunks, *refs):
    info = refs[0]
    packed = refs[1 : 1 + 2 * chunks]
    wg, wu, wd, cg, cu, cd = refs[1 + 2 * chunks : 7 + 2 * chunks]
    x_ref, g_ref, p_ref, place_ref, vg, vu, vd, sems = refs[7 + 2 * chunks :]
    rows = (packed[0].shape[0] - META) // 2
    hidden = wg.shape[2]
    copies = []
    for s in range(3):
        for src, extra, dst in ((wg, cg, vg), (wu, cu, vu), (wd, cd, vd)):
            copies.append((src.at[s] if s < 2 else extra.at[0], dst.at[s]))
    copies = fetch(copies, sems)
    numbers = copy_numbers(info[0], shadow_count)
    width = cap * chunks
    for k in range(chunks):
        own, sib = packed[2 * k], packed[2 * k + 1]
        codes, gate = row_codes(routing(own, sib, rows), numbers)
        tok = jnp.concatenate([own[0:rows, :], sib[0:rows, :]], axis=0)
        grad = jnp.concatenate([own[rows : 2 * rows, :], sib[rows : 2 * rows, :]], axis=0)
        for s in range(3):
            place, inputs, grads = gather_rows(codes, gate, s, cap, tok, grad)
            at = s * width + k * cap
            place_ref[at : at + cap, :] = place
            x_ref[at : at + cap, :] = inputs
            g_ref[at : at + cap, :] = grads
    for s in range(3):
        at = s * width
        inputs, grads = x_ref[at : at + width, :], g_ref[at : at + width, :]
        copies[3 * s].wait()
        p_ref[at : at + width, 0:hidden] = jnp.dot(
            inputs, vg[s], preferred_element_type=jnp.float32
        ).astype(jnp.bfloat16)
        copies[3 * s + 1].wait()
        p_ref[at : at + width, hidden : 2 * hidden] = jnp.dot(
            inputs, vu[s], preferred_element_type=jnp.float32
        ).astype(jnp.bfloat16)
        copies[3 * s + 2].wait()
        p_ref[at : at + width, 2 * hidden : 3 * hidden] = lax.dot_general(
            grads, vd[s], NT, preferred_element_type=jnp.float32
        ).astype(jnp.bfloat16)


def backward_kernel(parts, cap, chunks, *refs):
    partial = refs[0:parts]
    place_ref, wg, wu, cg, cu = refs[parts : parts + 5]
    a_ref, s_ref, own_ref, sib_ref, vg, vu, total, sems = refs[parts + 5 :]
    hidden = wg.shape[2]
    rows = own_ref.shape[0] // chunks
    width = cap * chunks
    copies = []
    for s in range(3):
        for src, extra, dst in ((wg, cg, vg), (wu, cu, vu)):
            copies.append((src.at[s] if s < 2 else extra.at[0], dst.at[s]))
    copies = fetch(copies, sems)
    for s in range(3):
        at = s * width
        full = partial[0][at : at + width, :].astype(jnp.float32)
        for other in partial[1:]:
            full = full + other[at : at + width, :].astype(jnp.float32)
        gate, up, down = full[:, 0:hidden], full[:, hidden : 2 * hidden], full[:, 2 * hidden :]
        sig = 1.0 / (1.0 + jnp.exp(-gate))
        swish = gate * sig
        grad_up = (down * swish).astype(jnp.bfloat16)
        grad_gate = (down * up * sig * (1.0 + gate * (1.0 - sig))).astype(jnp.bfloat16)
        inner = (swish * up).astype(jnp.bfloat16)
        to, base = (a_ref, at) if s < 2 else (s_ref, 0)
        to[base : base + width, 0:hidden] = grad_gate
        to[base : base + width, hidden : 2 * hidden] = grad_up
        to[base : base + width, 2 * hidden : 3 * hidden] = inner
        copies[2 * s].wait()
        route = lax.dot_general(grad_gate, vg[s], NT, preferred_element_type=jnp.float32)
        copies[2 * s + 1].wait()
        route = route + lax.dot_general(grad_up, vu[s], NT, preferred_element_type=jnp.float32)
        route = route.astype(jnp.bfloat16)
        for k in range(chunks):
            part = lax.dot_general(
                place_ref[at + k * cap : at + (k + 1) * cap, :],
                route[k * cap : (k + 1) * cap],
                TN,
                preferred_element_type=jnp.float32,
            )
            if s == 0:
                total[k] = part
            elif s == 1:
                total[k] += part
            else:
                part = (total[k] + part).astype(jnp.bfloat16)
                own_ref[k * rows : (k + 1) * rows, :] = part[0:rows]
                sib_ref[k * rows : (k + 1) * rows, :] = part[rows : 2 * rows]


def weights_kernel(shadow_count, cap, sizes, *refs):
    count, groups = shadow_count, len(sizes)
    info = refs[0]
    refs = refs[1:]
    xs, gs, acts = refs[0:groups], refs[groups : 2 * groups], refs[2 * groups : 3 * groups]
    shadow_acts = refs[3 * groups : 3 * groups + 2]
    packed = refs[3 * groups + 2 : 3 * groups + 2 + 2 * count]
    og, ou, od, x_all, g_all, a_all, tg, tu, td = refs[3 * groups + 2 + 2 * count :]
    rows = (packed[0].shape[0] - META) // 2
    hidden = og.shape[2]
    mine = pl.program_id(0)
    at = 0
    for i, size in enumerate(sizes):
        x_all[at : at + size, :] = xs[i][...]
        g_all[at : at + size, :] = gs[i][...]
        a_all[at : at + size, :] = acts[i][...]
        at += size

    def products():
        x, g = x_all[...], g_all[...]
        return (
            lax.dot_general(x, a_all[:, 0:hidden], TN, preferred_element_type=jnp.float32),
            lax.dot_general(x, a_all[:, hidden : 2 * hidden], TN, preferred_element_type=jnp.float32),
            lax.dot_general(a_all[:, 2 * hidden :], g, TN, preferred_element_type=jnp.float32),
        )

    tg[...], tu[...], td[...] = products()
    for slot in range(2):

        @pl.when(info[4 + 2 * slot] == mine)
        def _(slot=slot):
            holder = info[5 + 2 * slot]
            numbers = jnp.full((8, 1), 2 * count + holder, jnp.int32).astype(jnp.float32)
            for k in range(count):
                own, sib = packed[2 * k], packed[2 * k + 1]
                codes, gate = row_codes(routing(own, sib, rows), numbers)
                tok = jnp.concatenate([own[0:rows, :], sib[0:rows, :]], axis=0)
                grad = jnp.concatenate([own[rows : 2 * rows, :], sib[rows : 2 * rows, :]], axis=0)
                _, inputs, grads = gather_rows(codes, gate, 0, cap, tok, grad)
                x_all[k * cap : (k + 1) * cap, :] = inputs
                g_all[k * cap : (k + 1) * cap, :] = grads
                start = pl.multiple_of((holder ^ info[0] ^ k) * cap, 16)
                a_all[k * cap : (k + 1) * cap, :] = shadow_acts[slot][pl.ds(start, cap), :]
            more_g, more_u, more_d = products()
            tg[...] += more_g
            tu[...] += more_u
            td[...] += more_d

    og[0] = tg[...].astype(jnp.bfloat16)
    ou[0] = tu[...].astype(jnp.bfloat16)
    od[0] = td[...].astype(jnp.bfloat16)


def shadow_patterns():
    found = []
    for code in range(256):
        owners = [(code >> (2 * j)) & 3 for j in range(4)]
        if any(owners[j] == j for j in range(4)):
            continue
        if sorted(owners.count(i) for i in range(4)) == [0, 0, 2, 2]:
            found.append(owners)
    return found


def shadow_moves(acts, owners, count):
    z = lax.axis_index("expert")
    if count != 4:
        whole = lax.all_gather(acts, "expert")
        slots = jnp.arange(count, dtype=jnp.int32)
        low = jnp.min(jnp.where(owners == z, slots, count - 1))
        high = jnp.max(jnp.where(owners == z, slots, 0))
        return (
            lax.dynamic_index_in_dim(whole, low, 0, keepdims=False),
            lax.dynamic_index_in_dim(whole, high, 0, keepdims=False),
        )
    branches, which = [], jnp.int32(0)
    for i, pattern in enumerate(shadow_patterns()):
        lows = [(pattern.index(o), o) for o in sorted(set(pattern))]
        highs = [(3 - pattern[::-1].index(o), o) for o in sorted(set(pattern))]

        def branch(x, lows=lows, highs=highs):
            return lax.ppermute(x, "expert", lows), lax.ppermute(x, "expert", highs)

        branches.append(branch)
        same = jnp.all(owners == jnp.array(pattern, jnp.int32))
        which = jnp.where(same, i, which)
    return lax.switch(which, branches, acts)


def chunk_groups(count):
    groups, at, size = [[0]], 1, 1
    while at < count:
        groups.append(list(range(at, min(count, at + size))))
        at += size
        size = max(size, at)
    return groups


def on_device(
    tokens,
    out_grad,
    expert_ids,
    gate_weights,
    shadow_expert,
    w_gate,
    w_up,
    w_down,
    copy_gate,
    copy_up,
    copy_down,
):
    bf16 = jnp.bfloat16
    rows, width = tokens.shape
    hidden = w_gate.shape[2]
    count, dp_count = lax.axis_size("expert"), lax.axis_size("dp")
    cap = -(-2 * max(2, 3 * rows // (2 * count)) // 16) * 16
    z, core = lax.axis_index("expert"), lax.axis_index("inner")
    owners = shadow_expert // 2
    slots = jnp.arange(count, dtype=jnp.int32)
    low = jnp.min(jnp.where(owners == z, slots, count - 1))
    high = jnp.max(jnp.where(owners == z, slots, 0))
    is_owner = jnp.any(owners == z)
    of_low = jnp.where(is_owner, jnp.sum(jnp.where(slots == low, shadow_expert, 0)) % 2, -1)
    of_high = jnp.where(is_owner, jnp.sum(jnp.where(slots == high, shadow_expert, 0)) % 2, -1)
    info = jnp.stack(
        [z, core, 2 * z + core, jnp.int32(0), of_low, low, of_high, high]
    ).astype(jnp.int32)
    meta = jnp.concatenate([expert_ids.astype(jnp.float32), gate_weights], axis=1).T

    shape = jax.ShapeDtypeStruct
    pack = call(
        functools.partial(pack_kernel, count),
        shape((2 * rows + META, width), bf16),
        [SCALARS, SCALARS, WHOLE, WHOLE, WHOLE],
        WHOLE,
        [],
        0,
        8 * rows * width,
    )
    own = [pack(info, shadow_expert, tokens, out_grad, meta)]
    for k in range(1, count):
        own.append(lax.ppermute(own[0], "expert", [(i, i ^ k) for i in range(count)]))
    swap = [(0, 1), (1, 0)]
    sib = [lax.ppermute(x, "inner", swap) for x in own]

    groups = chunk_groups(count)
    kept, returned = [], [None] * count
    for group in groups:
        chunks = len(group)
        size = cap * chunks
        forward = call(
            functools.partial(forward_kernel, count, cap, chunks),
            (
                shape((3 * size, width), bf16),
                shape((3 * size, width), bf16),
                shape((3 * size, 3 * hidden), bf16),
                shape((3 * size, 2 * rows), bf16),
            ),
            [SCALARS] + [WHOLE] * (2 * chunks) + [REMAIN] * 6,
            (WHOLE,) * 4,
            [
                pltpu.VMEM((3, width, hidden), bf16),
                pltpu.VMEM((3, width, hidden), bf16),
                pltpu.VMEM((3, hidden, width), bf16),
                pltpu.SemaphoreType.DMA((9,)),
            ],
            18 * size * width * hidden,
            18 * width * hidden + 20 * size * width,
        )
        packed = [a for k in group for a in (own[k], sib[k])]
        inputs, grads, partial, place = forward(
            info, *packed, w_gate, w_up, w_down, copy_gate, copy_up, copy_down
        )
        if dp_count == 2:
            partials = [partial, lax.ppermute(partial, "dp", swap)]
        else:
            partials = [lax.psum(partial, "dp")]
        backward = call(
            functools.partial(backward_kernel, len(partials), cap, chunks),
            (
                shape((2 * size, 3 * hidden), bf16),
                shape((size, 3 * hidden), bf16),
                shape((chunks * rows, width), bf16),
                shape((chunks * rows, width), bf16),
            ),
            [WHOLE] * (len(partials) + 1) + [REMAIN] * 4,
            (WHOLE,) * 4,
            [
                pltpu.VMEM((3, width, hidden), bf16),
                pltpu.VMEM((3, width, hidden), bf16),
                pltpu.VMEM((chunks, 2 * rows, width), jnp.float32),
                pltpu.SemaphoreType.DMA((6,)),
            ],
            12 * size * width * hidden,
            12 * width * hidden + 20 * size * width,
        )
        acts, shadow_acts, dx_own, dx_sib = backward(
            *partials, place, w_gate, w_up, copy_gate, copy_up
        )
        dx_other = lax.ppermute(dx_sib, "inner", swap)
        for i, k in enumerate(group):
            both = dx_own[i * rows : (i + 1) * rows].astype(jnp.float32) + dx_other[
                i * rows : (i + 1) * rows
            ].astype(jnp.float32)
            if k > 0:
                both = lax.ppermute(both.astype(bf16), "expert", [(i, i ^ k) for i in range(count)])
            returned[k] = both
        kept.append((inputs, grads, acts, shadow_acts))

    total = returned[0]
    for x in returned[1:]:
        total = total + x.astype(jnp.float32)
    grad_tokens = total.astype(bf16)

    shadow_rows = jnp.concatenate([k[3] for k in kept], axis=0)
    moved = shadow_moves(shadow_rows, owners, count)
    sizes = [cap * len(g) for g in groups]

    def part(size, columns):
        return pl.BlockSpec((size, columns), lambda e: (e, 0))

    every = cap * count
    weights = call(
        functools.partial(weights_kernel, count, cap, sizes),
        (
            shape((2, width, hidden), bf16),
            shape((2, width, hidden), bf16),
            shape((2, hidden, width), bf16),
        ),
        [SCALARS]
        + [part(s, width) for s in sizes] * 2
        + [part(s, 3 * hidden) for s in sizes]
        + [WHOLE] * (2 + 2 * count),
        (
            pl.BlockSpec((1, width, hidden), lambda e: (e, 0, 0)),
            pl.BlockSpec((1, width, hidden), lambda e: (e, 0, 0)),
            pl.BlockSpec((1, hidden, width), lambda e: (e, 0, 0)),
        ),
        [
            pltpu.VMEM((every, width), bf16),
            pltpu.VMEM((every, width), bf16),
            pltpu.VMEM((every, 3 * hidden), bf16),
            pltpu.VMEM((width, hidden), jnp.float32),
            pltpu.VMEM((width, hidden), jnp.float32),
            pltpu.VMEM((hidden, width), jnp.float32),
        ],
        24 * every * width * hidden,
        24 * width * hidden,
        grid=(2,),
    )
    grad_gate, grad_up, grad_down = weights(
        info,
        *[k[0] for k in kept],
        *[k[1] for k in kept],
        *[k[2] for k in kept],
        *moved,
        *[a for k in range(count) for a in (own[k], sib[k])],
    )
    return grad_tokens, grad_gate, grad_up, grad_down


def solution(mesh):
    return jax.shard_map(
        on_device,
        mesh=mesh,
        in_specs=(
            P(("groups", "expert", "inner"), "dp"),
            P(("groups", "expert", "inner"), "dp"),
            P(("groups", "expert", "inner"), None),
            P(("groups", "expert", "inner"), None),
            P(),
            P("expert", "dp", "inner"),
            P("expert", "dp", "inner"),
            P("expert", "inner", "dp"),
            P("expert", "dp", "inner"),
            P("expert", "dp", "inner"),
            P("expert", "inner", "dp"),
        ),
        out_specs=(
            P(("groups", "expert", "inner"), "dp"),
            P(("groups", "expert"), "dp", "inner"),
            P(("groups", "expert"), "dp", "inner"),
            P(("groups", "expert"), "inner", "dp"),
        ),
        check_vma=False,
    )
```

```python
import functools

import jax
import jax.numpy as jnp
from jax import lax
from jax.experimental import pallas as pl
from jax.experimental.pallas import tpu as pltpu
from jax.sharding import PartitionSpec as P

META = 16


def call(body, out_shape, in_specs, out_specs, scratch, **kw):
    return pl.pallas_call(
        body,
        out_shape=out_shape,
        in_specs=in_specs,
        out_specs=out_specs,
        scratch_shapes=scratch,
        compiler_params=pltpu.CompilerParams(vmem_limit_bytes=60 * 1024 * 1024),
        **kw,
    )


WHOLE = pl.BlockSpec(memory_space=pltpu.VMEM)
SCALARS = pl.BlockSpec(memory_space=pltpu.SMEM)
REMAIN = pl.BlockSpec(memory_space=pl.ANY)


def position():
    return lax.axis_index("expert"), lax.axis_index("inner")


def pack_kernel(shadow_count, shadow, tok_ref, grad_ref, ids_ref, gate_ref, out_ref, which_ref):
    rows = tok_ref.shape[0]
    out_ref[0:rows, :] = tok_ref[...]
    out_ref[rows : 2 * rows, :] = grad_ref[...]
    z, core = position()
    ids, gates = ids_ref[...].astype(jnp.float32), gate_ref[...]
    choice = lax.broadcasted_iota(jnp.int32, ids.shape, 0)
    place = (2 * z + core) * rows + lax.broadcasted_iota(jnp.int32, ids.shape, 1) + choice
    place = place.astype(jnp.float32)
    entry = [shadow[j] for j in range(shadow_count)]
    named = [ids == e.astype(jnp.float32) for e in entry]
    copies = jnp.ones(ids.shape, jnp.float32)
    for hit in named:
        copies = copies + jnp.where(hit, 1.0, 0.0)
    halves = place - 2.0 * jnp.floor((place + 0.5) * 0.5)
    thirds = place - 3.0 * jnp.floor((place + 0.5) * (1.0 / 3.0))
    chosen = jnp.where(copies == 2.0, halves, jnp.where(copies == 3.0, thirds, 0.0))
    serving = ids
    for j in range(shadow_count):
        before = jnp.int32(0)
        for i in range(j):
            before = before + jnp.where(entry[i] == entry[j], 1, 0)
        take = named[j] & (chosen == (before + 1).astype(jnp.float32))
        serving = jnp.where(take, float(2 * shadow_count + j), serving)
    high = gates.astype(jnp.bfloat16)
    rest = gates - high.astype(jnp.float32)
    middle = rest.astype(jnp.bfloat16)
    low = (rest - middle.astype(jnp.float32)).astype(jnp.bfloat16)
    block = jnp.concatenate(
        [
            serving,
            high.astype(jnp.float32),
            middle.astype(jnp.float32),
            low.astype(jnp.float32),
            jnp.zeros((META - 8, rows), jnp.float32),
        ],
        axis=0,
    )
    out_ref[2 * rows : 2 * rows + META, :] = jnp.zeros((META, tok_ref.shape[1]), jnp.bfloat16)
    out_ref[2 * rows : 2 * rows + META, 0:rows] = block.astype(jnp.bfloat16)
    which = jnp.int32(0)
    if shadow_count == 4:
        for i, (_, placements) in enumerate(shadow_moves()):
            for owners in placements:
                same = jnp.bool_(True)
                for j in range(4):
                    same = same & (entry[j] // 2 == owners[j])
                which = jnp.where(same, i, which)
    which_ref[0] = which


def routing(meta):
    meta = meta.astype(jnp.float32)
    return meta[0:1], meta[1:2], meta[2:3] + meta[4:5] + meta[6:7], meta[3:4] + meta[5:6] + meta[7:8]


def row_codes(meta, numbers):
    first, second, gate_a, gate_b = meta
    tokens = first.shape[1]
    hit_a, hit_b = first == numbers, second == numbers
    hit = jnp.where(hit_a | hit_b, 1.0, 0.0)
    gate = jnp.where(hit_a, gate_a, 0.0) + jnp.where(hit_b, gate_b, 0.0)
    earlier = lax.broadcasted_iota(jnp.int32, (tokens, tokens), 0) < lax.broadcasted_iota(
        jnp.int32, (tokens, tokens), 1
    )
    rank = jnp.dot(
        hit.astype(jnp.bfloat16),
        jnp.where(earlier, 1.0, 0.0).astype(jnp.bfloat16),
        preferred_element_type=jnp.float32,
    )
    return jnp.where(hit > 0.0, rank, -1.0), gate


def gather_rows(codes, gate, wanted, cap, tok, grad):
    tokens = codes.shape[1]
    row = lax.broadcasted_iota(jnp.int32, (cap, tokens), 0).astype(jnp.float32)
    places, gates = [], []
    for s in wanted:
        place = row == codes[s : s + 1, :]
        gates.append(
            jnp.sum(jnp.where(place, gate[s : s + 1, :], 0.0), axis=1, keepdims=True)
        )
        places.append(jnp.where(place, 1.0, 0.0).astype(jnp.bfloat16))
    place = places[0] if len(places) == 1 else jnp.concatenate(places, axis=0)
    row_gate = gates[0] if len(gates) == 1 else jnp.concatenate(gates, axis=0)
    inputs = jnp.dot(place, tok, preferred_element_type=jnp.float32).astype(jnp.bfloat16)
    grads = jnp.dot(place, grad, preferred_element_type=jnp.float32)
    return place, inputs, (grads * row_gate).astype(jnp.bfloat16)


def held_for(shadow, count):
    z = position()[0]
    near, far = jnp.int32(0), jnp.int32(0)
    for k in range(1, count):
        mine = shadow[z ^ k] // 2 == z
        near = jnp.where(mine & (near == 0), k, near)
        far = jnp.where(mine, k, far)
    found = near > 0
    return tuple(
        (z ^ k, jnp.where(found, shadow[z ^ k] - 2 * z, -1)) for k in (near, far)
    )


def copy_numbers(shadow, count):
    z = position()[0]
    slot = lax.broadcasted_iota(jnp.int32, (8, 1), 0)
    number = jnp.where(slot < 2, 2 * z + slot, jnp.where(slot == 2, 2 * count + z, -1))
    for i, (holder, of) in enumerate(held_for(shadow, count)):
        number = jnp.where(slot == 3 + i, jnp.where(of >= 0, 2 * count + holder, -1), number)
    return number.astype(jnp.float32)


def heavy_loads(meta, count, light):
    holder = lax.broadcasted_iota(jnp.int32, (-(-count // 8) * 8, 1), 0)
    number = jnp.where(holder < count, 2 * count + holder, -1).astype(jnp.float32)
    mine = jnp.where(meta[0] == number, 1.0, 0.0) + jnp.where(meta[1] == number, 1.0, 0.0)
    load = jnp.sum(mine, axis=1, keepdims=True)
    return jnp.sum(jnp.where(load > float(light), 1.0, 0.0), axis=0, keepdims=True)


NT = (((1,), (1,)), ((), ()))
TN = (((0,), (0,)), ((), ()))


class Copies:
    def __init__(self, sems):
        self.sems, self.started = sems, []

    def start(self, src, dst):
        copy = pltpu.make_async_copy(src, dst, self.sems.at[len(self.started)])
        copy.start()
        self.started.append(copy)
        return copy


def blocks_of(size):
    block = min(256, size)
    return block, size // block


def forward_kernel(count, cap, light, split, shadow, load_in, own, sib, *refs):
    weights, load_out, outs, scratch = refs[0:6], refs[6], refs[7 : 11 + split], refs[11 + split :]
    vg, vu, vd, rows_in, rows_out, meta, x_s, g_s, p_s, place_s, sems = scratch
    rows, hidden = rows_in.shape[0] // 2, vg.shape[2]
    copies = Copies(sems)
    loads = []
    for core, src in enumerate((own, sib)):
        at = pl.ds(core * rows, rows)
        loads.append(copies.start(src.at[pl.ds(2 * rows, META), pl.ds(0, rows)], meta.at[:, at]))
        loads.append(copies.start(src.at[pl.ds(0, rows)], rows_in.at[at]))
        loads.append(copies.start(src.at[pl.ds(rows, rows)], rows_out.at[at]))
    for load in loads:
        load.wait()
    ready = {}
    for s in range(3):
        for i, (src, extra, dst) in enumerate(zip(weights[0:3], weights[3:6], (vg, vu, vd))):
            ready[3 * s + i] = copies.start(src.at[s] if s < 2 else extra.at[0], dst.at[s])
    routes = routing(meta[...])
    load_out[...] = load_in[...] + heavy_loads(routes, count, light)
    codes, gate = row_codes(routes, copy_numbers(shadow, count))
    place, x_s[...], g_s[...] = gather_rows(
        codes, gate, range(5), cap, rows_in[...], rows_out[...]
    )
    place_s[...] = place[0 : 3 * cap]
    stores = [copies.start(a, b) for a, b in zip((x_s, g_s, place_s), (outs[0], outs[1], outs[2]))]
    for s in range(3):
        at = slice(s * cap, (s + 1) * cap)
        inputs, grads = x_s[at, :], g_s[at, :]
        ready[3 * s].wait()
        p_s[at, 0:hidden] = jnp.dot(
            inputs, vg[s], preferred_element_type=jnp.float32
        ).astype(jnp.bfloat16)
        ready[3 * s + 1].wait()
        p_s[at, hidden : 2 * hidden] = jnp.dot(
            inputs, vu[s], preferred_element_type=jnp.float32
        ).astype(jnp.bfloat16)
        ready[3 * s + 2].wait()
        p_s[at, 2 * hidden :] = lax.dot_general(
            grads, vd[s], NT, preferred_element_type=jnp.float32
        ).astype(jnp.bfloat16)
        of = pl.ds(s * cap, cap)
        stores.append(copies.start(p_s.at[of], outs[4] if split and s == 2 else outs[3].at[of]))
    for store in stores:
        store.wait()


def choose_kernel(moves, which, load, other, last):
    heavy = jnp.max(load[...] + other[...]) > 0.0
    last[0] = which[0] + jnp.where(heavy, moves, 0)


def activation(partial, hidden):
    full = partial[0].astype(jnp.float32)
    for other in partial[1:]:
        full = full + other.astype(jnp.float32)
    gate, up, down = full[:, 0:hidden], full[:, hidden : 2 * hidden], full[:, 2 * hidden :]
    sig = 1.0 / (1.0 + jnp.exp(-gate))
    swish = gate * sig
    return (
        (down * up * sig * (1.0 + gate * (1.0 - sig))).astype(jnp.bfloat16),
        (down * swish).astype(jnp.bfloat16),
        (swish * up).astype(jnp.bfloat16),
    )


def token_grads(grad_gate, grad_up, place, gate_weight, up_weight):
    route = lax.dot_general(grad_gate, gate_weight, NT, preferred_element_type=jnp.float32)
    route = route + lax.dot_general(grad_up, up_weight, NT, preferred_element_type=jnp.float32)
    return lax.dot_general(
        place, route.astype(jnp.bfloat16), TN, preferred_element_type=jnp.float32
    )


def backward_kernel(parts, split, cap, light, carried, *refs):
    pieces = 2 if split else 1
    partial = [refs[pieces * i : pieces * (i + 1)] for i in range(parts)]
    refs = refs[pieces * parts :]
    place_in, weights, carry, refs = refs[0], refs[1:5], refs[5 : 5 + carried], refs[5 + carried :]
    kinds = 2 if light < cap else 1
    a_out, shadow_outs, own_out, sib_out = refs[0], refs[1 : 1 + kinds], *refs[1 + kinds : 3 + kinds]
    vg, vu, part_s, place_s, a_s, total, own_s, sib_s, sems = refs[3 + kinds :]
    hidden, rows = vg.shape[2], own_s.shape[0]
    copies = Copies(sems)
    loads, ready, stores, ends = [], [], [], [0, 0]
    for s in range(3):
        of = pl.ds(s * cap, cap)
        loads.append([])
        for i, p in enumerate(partial):
            src = p[1] if split and s == 2 else p[0].at[of]
            loads[s].append(copies.start(src, part_s.at[i, of]))
        loads[s].append(copies.start(place_in.at[of], place_s.at[of]))
        for src, extra, dst in zip(weights[0:2], weights[2:4], (vg, vu)):
            ready.append(copies.start(src.at[s] if s < 2 else extra.at[0], dst.at[s]))
    for kind, held in enumerate(carry):
        kind = kind + kinds - carried
        ends[kind] = held.shape[0]
        stores.append(copies.start(held, shadow_outs[kind].at[pl.ds(0, ends[kind])]))
    for s in range(3):
        at, of = slice(s * cap, (s + 1) * cap), pl.ds(s * cap, cap)
        for load in loads[s]:
            load.wait()
        grads = activation([part_s[i, at, :] for i in range(parts)], hidden)
        for i in range(3):
            a_s[at, i * hidden : (i + 1) * hidden] = grads[i]
        if s < 2:
            stores.append(copies.start(a_s.at[of], a_out.at[of]))
        else:
            first = 2 * cap
            for kind, size in enumerate((light, cap - light)[0:kinds]):
                to = shadow_outs[kind].at[pl.ds(ends[kind], size)]
                stores.append(copies.start(a_s.at[pl.ds(first, size)], to))
                first += size
        ready[2 * s].wait()
        ready[2 * s + 1].wait()
        part = token_grads(grads[0], grads[1], place_s[at, :], vg[s], vu[s])
        if s == 0:
            total[...] = part
        elif s == 1:
            total[...] += part
        else:
            part = total[...] + part
            own_s[...] = part[0:rows].astype(jnp.bfloat16)
            sib_s[...] = part[rows : 2 * rows].astype(jnp.bfloat16)
            stores.append(copies.start(own_s, own_out))
            stores.append(copies.start(sib_s, sib_out))
    for store in stores:
        store.wait()


def weights_kernel(count, cap, light, pieces, heavy_from, shadow, which, *refs):
    arrays = sum(n for _, n in pieces)
    owned, whole, near = cap * count, cap * count, light * count
    xs, gs, acts = refs[0:count], refs[count : 2 * count], refs[2 * count : 3 * count]
    refs = refs[3 * count :]
    shadow_acts = refs[0:arrays]
    og, ou, od, x_all, g_all, a_all, og_s, ou_s, od_s, sems, slot_sems = refs[arrays:]
    width, hidden = og_s.shape[1], og_s.shape[2]

    def owned_copies(e):
        copies = []
        for i in range(count):
            to, of = pl.ds(i * cap, cap), pl.ds(pl.multiple_of(e * cap, 16), cap)
            for j, (srcs, dst) in enumerate(((xs, x_all), (gs, g_all), (acts, a_all))):
                sem = sems.at[e * 3 * count + 3 * i + j]
                copies.append(pltpu.make_async_copy(srcs[i].at[of], dst.at[e, to], sem))
        return copies

    for e in range(2):
        for copy in owned_copies(e):
            copy.start()
    heavy = which[0] >= heavy_from
    held = held_for(shadow, count)
    together = held[0][1] == held[1][1]
    after_first = jnp.where(together, jnp.where(heavy, whole, near), 0)

    def slot_copies(slot, act):
        e = jnp.maximum(held[slot][1], 0)
        start = owned if slot == 0 else owned + after_first
        z, found = position()[0], held[slot][1] >= 0
        rest, first = cap - light, (3 + slot) * cap
        plans = []
        for k in range(count):
            part = held[slot][0] ^ z ^ k
            for src, dst in ((xs[k], x_all), (gs[k], g_all)):
                plans.append((found, src.at[pl.ds(first, light)], dst, part * light, light))
                if rest:
                    src = src.at[pl.ds(first + light, rest)]
                    plans.append((found & heavy, src, dst, near + part * rest, rest))
        at, i = 0, 0
        for size, number in pieces:
            for n in range(number):
                when = found if at < near else found & heavy
                if number == count - 1:
                    when = when & ((held[slot][0] ^ z) == n + 1)
                if number == count - 1 or n == slot:
                    plans.append((when, shadow_acts[i], a_all, at, size))
                i += 1
            at += size
        for number, (when, src, dst, at, size) in enumerate(plans):
            to = pl.ds(pl.multiple_of(start + at, 16), size)
            sem = slot_sems.at[slot, number]

            @pl.when(when)
            def _(src=src, dst=dst, to=to, sem=sem):
                act(pltpu.make_async_copy(src, dst.at[e, to], sem))

    def for_slots(act):
        for slot in range(2):
            slot_copies(slot, act)

    for_slots(lambda copy: copy.start())
    f_block, f_blocks = blocks_of(width)
    h_block, h_blocks = blocks_of(hidden)

    def products(e, k):
        for j in range(f_blocks):
            of = slice(j * f_block, (j + 1) * f_block)
            both = lax.dot_general(
                x_all[e, 0:k, of],
                a_all[e, 0:k, 0 : 2 * hidden],
                TN,
                preferred_element_type=jnp.float32,
            ).astype(jnp.bfloat16)
            og_s[e, of, :] = both[:, 0:hidden]
            ou_s[e, of, :] = both[:, hidden:]
        for j in range(h_blocks):
            of = slice(j * h_block, (j + 1) * h_block)
            from_ = slice(2 * hidden + j * h_block, 2 * hidden + (j + 1) * h_block)
            od_s[e, of, :] = lax.dot_general(
                a_all[e, 0:k, from_], g_all[e, 0:k, :], TN, preferred_element_type=jnp.float32
            ).astype(jnp.bfloat16)

    def results(e):
        return [
            pltpu.make_async_copy(src.at[e], dst.at[e], sems.at[e * 3 * count + i])
            for i, (src, dst) in enumerate(((og_s, og), (ou_s, ou), (od_s, od)))
        ]

    def turn(n, _):
        e = jnp.where(held[0][1] == 0, 1 - n, n)
        for copy in owned_copies(e):
            copy.wait()

        @pl.when(n == jnp.where(together, 1, 0))
        def _():
            for_slots(lambda copy: copy.wait())

        first = jnp.where(held[0][1] == e, 1, 0)
        slots = first + jnp.where(held[1][1] == e, 1, 0)

        @pl.when(slots == 0)
        def _():
            products(e, owned)

        for number in (1, 2):
            if near < whole:

                @pl.when((slots == number) & ~heavy)
                def _(number=number):
                    products(e, owned + number * near)

            @pl.when((slots == number) & heavy)
            def _(number=number):
                products(e, owned + number * whole)

        for copy in results(e):
            copy.start()
        return 0

    lax.fori_loop(0, 2, turn, 0)
    for e in range(2):
        for copy in results(e):
            copy.wait()


def shadow_moves():
    moves = {}
    for code in range(256):
        owners = [(code >> (2 * j)) & 3 for j in range(4)]
        if any(owners[j] == j for j in range(4)):
            continue
        if sorted(owners.count(i) for i in range(4)) != [0, 0, 2, 2]:
            continue
        apart = sorted({j ^ owners[j] for j in range(4)})
        if 1 in apart:
            perms = [[(j, j ^ d) for j in range(4)] for d in apart]
        else:
            perms = [[(j, o) for j, o in enumerate(owners) if j ^ o == d] for d in apart]
        key = tuple(tuple(p) for p in perms)
        moves.setdefault(key, []).append(owners)
    return list(moves.items())


def after(value, *others):
    return lax.optimization_barrier((value, *others))[0]


def on_device(
    tokens,
    out_grad,
    expert_ids,
    gate_weights,
    shadow_expert,
    w_gate,
    w_up,
    w_down,
    copy_gate,
    copy_up,
    copy_down,
):
    bf16 = jnp.bfloat16
    rows, width = tokens.shape
    hidden = w_gate.shape[2]
    count, dp_count = lax.axis_size("expert"), lax.axis_size("dp")
    cap = -(-2 * max(2, 3 * rows // (2 * count)) // 16) * 16
    light = -(-2 * cap // 3 // 16) * 16
    swap = [(0, 1), (1, 0)]
    shape = jax.ShapeDtypeStruct

    def to_index(x, k):
        return lax.ppermute(x, "expert", [(i, i ^ k) for i in range(count)])

    def swapped(x):
        return lax.ppermute(x, "inner", swap)

    def forward(load, own, sib, split=0):
        outs = (
            shape((8, 128), jnp.float32),
            shape((5 * cap, width), bf16),
            shape((5 * cap, width), bf16),
            shape((3 * cap, 2 * rows), bf16),
            *[shape((n * cap, 3 * hidden), bf16) for n in ((2, 1) if split else (3,))],
        )
        return call(
            functools.partial(forward_kernel, count, cap, light, split),
            outs,
            [SCALARS, WHOLE] + [REMAIN] * 8,
            (WHOLE,) + (REMAIN,) * (len(outs) - 1),
            [
                pltpu.VMEM((3, width, hidden), bf16),
                pltpu.VMEM((3, width, hidden), bf16),
                pltpu.VMEM((3, hidden, width), bf16),
                pltpu.VMEM((2 * rows, width), bf16),
                pltpu.VMEM((2 * rows, width), bf16),
                pltpu.VMEM((META, 2 * rows), bf16),
                pltpu.VMEM((5 * cap, width), bf16),
                pltpu.VMEM((5 * cap, width), bf16),
                pltpu.VMEM((3 * cap, 3 * hidden), bf16),
                pltpu.VMEM((3 * cap, 2 * rows), bf16),
                pltpu.SemaphoreType.DMA((21,)),
            ],
        )(shadow_expert, load, own, sib, w_gate, w_up, w_down, copy_gate, copy_up, copy_down)

    def exchange(partial):
        if dp_count == 2:
            return [partial, lax.ppermute(partial, "dp", swap)]
        return [lax.psum(partial, "dp")]

    def backward(partials, place, carry=(), near=1, far=1):
        parts, split = len(partials), len(partials[0]) - 1
        outs = [shape((2 * cap, 3 * hidden), bf16), shape((near * light, 3 * hidden), bf16)]
        if light < cap:
            outs.append(shape((far * (cap - light), 3 * hidden), bf16))
        outs += [shape((rows, width), bf16)] * 2
        return call(
            functools.partial(backward_kernel, parts, split, cap, light, len(carry)),
            outs,
            [REMAIN] * ((1 + split) * parts + 5 + len(carry)),
            [REMAIN] * len(outs),
            [
                pltpu.VMEM((3, width, hidden), bf16),
                pltpu.VMEM((3, width, hidden), bf16),
                pltpu.VMEM((parts, 3 * cap, 3 * hidden), bf16),
                pltpu.VMEM((3 * cap, 2 * rows), bf16),
                pltpu.VMEM((3 * cap, 3 * hidden), bf16),
                pltpu.VMEM((2 * rows, width), jnp.float32),
                pltpu.VMEM((rows, width), bf16),
                pltpu.VMEM((rows, width), bf16),
                pltpu.SemaphoreType.DMA((17 + 3 * parts,)),
            ],
        )(*[p for x in partials for p in x], place, w_gate, w_up, copy_gate, copy_up, *carry)

    def give_back(dx_own, dx_sib, k):
        both = dx_own.astype(jnp.float32) + swapped(dx_sib).astype(jnp.float32)
        return to_index(both.astype(bf16), k) if k else both

    def add_up(returned):
        total = returned[0]
        for x in returned[1:]:
            total = total + x.astype(jnp.float32)
        return total.astype(bf16)

    def weight_grads(kept, pieces, which, heavy_from):
        layout = [(p[0].shape[0], len(p)) for p in pieces]
        outs = (
            shape((2, width, hidden), bf16),
            shape((2, width, hidden), bf16),
            shape((2, hidden, width), bf16),
        )
        most = cap * count * 3
        arrays = [
            *[k[0] for k in kept],
            *[k[1] for k in kept],
            *[k[2] for k in kept],
            *[x for p in pieces for x in p],
        ]
        return call(
            functools.partial(weights_kernel, count, cap, light, layout, heavy_from),
            outs,
            [SCALARS, SCALARS] + [REMAIN] * len(arrays),
            (REMAIN,) * 3,
            [
                pltpu.VMEM((2, most, width), bf16),
                pltpu.VMEM((2, most, width), bf16),
                pltpu.VMEM((2, most, 3 * hidden), bf16),
                *[pltpu.VMEM(o.shape, bf16) for o in outs],
                pltpu.SemaphoreType.DMA((6 * count,)),
                pltpu.SemaphoreType.DMA((2, 4 * count + sum(n for _, n in layout))),
            ],
        )(shadow_expert, which, *arrays)

    own, which = call(
        functools.partial(pack_kernel, count),
        (shape((2 * rows + META, width), bf16), shape((1,), jnp.int32)),
        [SCALARS] + [WHOLE] * 4,
        (WHOLE, SCALARS),
        [],
    )(shadow_expert, tokens, out_grad, expert_ids.T, gate_weights.T)
    load = jnp.zeros((8, 128), jnp.float32)
    if count != 4:
        kept, returned, shadow_acts = [], [], []
        for k in range(count):
            here = to_index(own, k) if k else own
            sib = swapped(here)
            load, inputs, grads, place, partial = forward(load, here, sib)
            acts, *shadow_part, dx_own, dx_sib = backward([[p] for p in exchange(partial)], place)
            returned.append(give_back(dx_own, dx_sib, k))
            kept.append((inputs, grads, acts))
            shadow_acts += shadow_part
        whole = lax.all_gather(jnp.concatenate(shadow_acts, axis=0), "expert")
        z = lax.axis_index("expert")
        apart = jnp.arange(count, dtype=jnp.int32) ^ z
        held = shadow_expert // 2 == z
        near = jnp.min(jnp.where(held, apart, count - 1))
        far = jnp.max(jnp.where(held, apart, 0))
        near = lax.dynamic_index_in_dim(whole, z ^ near, 0, keepdims=False)
        far = lax.dynamic_index_in_dim(whole, z ^ far, 0, keepdims=False)
        pieces = [[near, far]]
        return (add_up(returned), *weight_grads(kept, pieces, which, 0))

    moves = [perms for perms, _ in shadow_moves()]

    def everywhere(x):
        two = to_index(x, 2)
        return [to_index(x, 1), two, to_index(two, 1)]

    here1 = to_index(own, 1)
    sib0 = swapped(own)
    load, x0, g0, place0, p0, q0 = forward(load, own, sib0, 1)
    t0 = lax.ppermute(q0, "dp", swap)
    r0 = lax.ppermute(p0, "dp", swap)
    here2 = to_index(after(own, q0), 2)
    sib1 = swapped(after(here1, t0))
    load, x1, g1, place1, p1, q1 = forward(load, here1, sib1, 1)
    p1, q1 = after((p1, q1), r0)
    t1 = lax.ppermute(q1, "dp", swap)
    r1 = lax.ppermute(p1, "dp", swap)
    here3 = to_index(here2, 1)
    a0, near0, far0, dx_own0, dx_sib0 = backward([[p0, q0], [after(r0, p1), t0]], place0)
    sib2 = swapped(after(here2, a0, t1))
    moved0 = everywhere(near0)
    ret0 = give_back(dx_own0, dx_sib0, 0)
    load, x2, g2, place2, p2, q2 = forward(load, here2, sib2, 1)
    p2, q2 = after((p2, q2), r1)
    t2 = lax.ppermute(q2, "dp", swap)
    r2 = lax.ppermute(p2, "dp", swap)
    a1, near1, far01, dx_own1, dx_sib1 = backward(
        [[p1, q1], [after(r1, p2), t1]], place1, (far0,), 1, 2
    )
    sib3 = swapped(after(here3, a1, t2, moved0[0], moved0[1]))
    moved1 = everywhere(near1)
    ret1 = give_back(dx_own1, dx_sib1, 1)
    load, x3, g3, place3, p3, q3 = forward(load, here3, sib3, 1)
    p3, q3 = after((p3, q3), r2, moved0[2], moved1[0], moved1[1])
    t3 = lax.ppermute(q3, "dp", swap)
    r3 = lax.ppermute(p3, "dp", swap)
    last = call(
        functools.partial(choose_kernel, len(moves)),
        shape((1,), jnp.int32),
        [SCALARS, WHOLE, WHOLE],
        SCALARS,
        [],
    )(which, load, lax.ppermute(load, "groups", swap))
    a2, near2, far012, dx_own2, dx_sib2 = backward(
        [[p2, q2], [after(r2, p3), t2]], place2, (far01,), 1, 3
    )
    moved2 = lax.switch(
        which[0],
        [functools.partial(lambda m, x: [lax.ppermute(x, "expert", p) for p in m], m) for m in moves],
        after(near2, t3, moved1[2]),
    )
    ret2 = give_back(dx_own2, dx_sib2, 2)
    r3 = after(r3, ret1, moved2)
    a3, near3, rest, dx_own3, dx_sib3 = backward([[p3, q3], [r3, t3]], place3, (far012,), 1, 4)
    near3 = after(near3, ret2)

    def light_branch(perms, x, more):
        return [[lax.ppermute(x, "expert", p), more] for p in perms]

    def heavy_branch(perms, x, more):
        return [[lax.ppermute(y, "expert", p) for y in (x, more)] for p in perms]

    moved3 = lax.switch(
        last[0],
        [functools.partial(f, m) for f in (light_branch, heavy_branch) for m in moves],
        near3,
        rest,
    )
    ret3 = give_back(dx_own3, dx_sib3, 3)
    pieces = [moved0, moved1, moved2, [m[0] for m in moved3], [m[1] for m in moved3]]
    kept = [(x0, g0, a0), (x1, g1, a1), (x2, g2, a2), (x3, g3, a3)]
    grads = weight_grads(kept, pieces, last, len(moves))
    return (add_up([ret0, ret1, ret2, ret3]), *grads)


def solution(mesh):
    return jax.shard_map(
        on_device,
        mesh=mesh,
        in_specs=(
            P(("groups", "expert", "inner"), "dp"),
            P(("groups", "expert", "inner"), "dp"),
            P(("groups", "expert", "inner"), None),
            P(("groups", "expert", "inner"), None),
            P(),
            P("expert", "dp", "inner"),
            P("expert", "dp", "inner"),
            P("expert", "inner", "dp"),
            P("expert", "dp", "inner"),
            P("expert", "dp", "inner"),
            P("expert", "inner", "dp"),
        ),
        out_specs=(
            P(("groups", "expert", "inner"), "dp"),
            P(("groups", "expert"), "dp", "inner"),
            P(("groups", "expert"), "dp", "inner"),
            P(("groups", "expert"), "inner", "dp"),
        ),
        check_vma=False,
    )
```

```python
import functools

import jax
import jax.numpy as jnp
from jax import lax
from jax.experimental import pallas as pl
from jax.experimental.pallas import tpu as pltpu
from jax.sharding import PartitionSpec as P

META = 16


def call(body, out_shape, in_specs, out_specs, scratch, **kw):
    return pl.pallas_call(
        body,
        out_shape=out_shape,
        in_specs=in_specs,
        out_specs=out_specs,
        scratch_shapes=scratch,
        compiler_params=pltpu.CompilerParams(vmem_limit_bytes=60 * 1024 * 1024),
        **kw,
    )


WHOLE = pl.BlockSpec(memory_space=pltpu.VMEM)
SCALARS = pl.BlockSpec(memory_space=pltpu.SMEM)
REMAIN = pl.BlockSpec(memory_space=pl.ANY)


def position():
    return lax.axis_index("expert"), lax.axis_index("inner")


def pack_kernel(shadow_count, shadow, tok_ref, grad_ref, ids_ref, gate_ref, out_ref, which_ref):
    rows = tok_ref.shape[0]
    out_ref[0:rows, :] = tok_ref[...]
    out_ref[rows : 2 * rows, :] = grad_ref[...]
    z, core = position()
    ids, gates = ids_ref[...].astype(jnp.float32), gate_ref[...]
    choice = lax.broadcasted_iota(jnp.int32, ids.shape, 0)
    place = (2 * z + core) * rows + lax.broadcasted_iota(jnp.int32, ids.shape, 1) + choice
    place = place.astype(jnp.float32)
    entry = [shadow[j] for j in range(shadow_count)]
    named = [ids == e.astype(jnp.float32) for e in entry]
    copies = jnp.ones(ids.shape, jnp.float32)
    for hit in named:
        copies = copies + jnp.where(hit, 1.0, 0.0)
    halves = place - 2.0 * jnp.floor((place + 0.5) * 0.5)
    thirds = place - 3.0 * jnp.floor((place + 0.5) * (1.0 / 3.0))
    chosen = jnp.where(copies == 2.0, halves, jnp.where(copies == 3.0, thirds, 0.0))
    serving = ids
    for j in range(shadow_count):
        before = jnp.int32(0)
        for i in range(j):
            before = before + jnp.where(entry[i] == entry[j], 1, 0)
        take = named[j] & (chosen == (before + 1).astype(jnp.float32))
        serving = jnp.where(take, float(2 * shadow_count + j), serving)
    high = gates.astype(jnp.bfloat16)
    rest = gates - high.astype(jnp.float32)
    middle = rest.astype(jnp.bfloat16)
    low = (rest - middle.astype(jnp.float32)).astype(jnp.bfloat16)
    block = jnp.concatenate(
        [
            serving,
            high.astype(jnp.float32),
            middle.astype(jnp.float32),
            low.astype(jnp.float32),
            jnp.zeros((META - 8, rows), jnp.float32),
        ],
        axis=0,
    )
    out_ref[2 * rows : 2 * rows + META, :] = jnp.zeros((META, tok_ref.shape[1]), jnp.bfloat16)
    out_ref[2 * rows : 2 * rows + META, 0:rows] = block.astype(jnp.bfloat16)
    which = jnp.int32(0)
    if shadow_count == 4:
        for i, (_, placements) in enumerate(shadow_moves()):
            for owners in placements:
                same = jnp.bool_(True)
                for j in range(4):
                    same = same & (entry[j] // 2 == owners[j])
                which = jnp.where(same, i, which)
    which_ref[0] = which


def routing(meta):
    meta = meta.astype(jnp.float32)
    return meta[0:1], meta[1:2], meta[2:3] + meta[4:5] + meta[6:7], meta[3:4] + meta[5:6] + meta[7:8]


def row_codes(meta, numbers):
    first, second, gate_a, gate_b = meta
    tokens = first.shape[1]
    hit_a, hit_b = first == numbers, second == numbers
    hit = jnp.where(hit_a | hit_b, 1.0, 0.0)
    gate = jnp.where(hit_a, gate_a, 0.0) + jnp.where(hit_b, gate_b, 0.0)
    earlier = lax.broadcasted_iota(jnp.int32, (tokens, tokens), 0) < lax.broadcasted_iota(
        jnp.int32, (tokens, tokens), 1
    )
    rank = jnp.dot(
        hit.astype(jnp.bfloat16),
        jnp.where(earlier, 1.0, 0.0).astype(jnp.bfloat16),
        preferred_element_type=jnp.float32,
    )
    return jnp.where(hit > 0.0, rank, -1.0), gate


def gather_rows(codes, gate, wanted, cap, tok, grad):
    tokens = codes.shape[1]
    row = lax.broadcasted_iota(jnp.int32, (cap, tokens), 0).astype(jnp.float32)
    places, gates = [], []
    for s in wanted:
        place = row == codes[s : s + 1, :]
        gates.append(
            jnp.sum(jnp.where(place, gate[s : s + 1, :], 0.0), axis=1, keepdims=True)
        )
        places.append(jnp.where(place, 1.0, 0.0).astype(jnp.bfloat16))
    place = places[0] if len(places) == 1 else jnp.concatenate(places, axis=0)
    row_gate = gates[0] if len(gates) == 1 else jnp.concatenate(gates, axis=0)
    inputs = jnp.dot(place, tok, preferred_element_type=jnp.float32).astype(jnp.bfloat16)
    grads = jnp.dot(place, grad, preferred_element_type=jnp.float32)
    return place, inputs, (grads * row_gate).astype(jnp.bfloat16)


def held_for(shadow, count):
    z = position()[0]
    near, far = jnp.int32(0), jnp.int32(0)
    for k in range(1, count):
        mine = shadow[z ^ k] // 2 == z
        near = jnp.where(mine & (near == 0), k, near)
        far = jnp.where(mine, k, far)
    found = near > 0
    return tuple(
        (z ^ k, jnp.where(found, shadow[z ^ k] - 2 * z, -1)) for k in (near, far)
    )


def copy_numbers(shadow, count):
    z = position()[0]
    slot = lax.broadcasted_iota(jnp.int32, (8, 1), 0)
    number = jnp.where(slot < 2, 2 * z + slot, jnp.where(slot == 2, 2 * count + z, -1))
    for i, (holder, of) in enumerate(held_for(shadow, count)):
        number = jnp.where(slot == 3 + i, jnp.where(of >= 0, 2 * count + holder, -1), number)
    return number.astype(jnp.float32)


def heavy_loads(meta, count, light):
    holder = lax.broadcasted_iota(jnp.int32, (-(-count // 8) * 8, 1), 0)
    number = jnp.where(holder < count, 2 * count + holder, -1).astype(jnp.float32)
    mine = jnp.where(meta[0] == number, 1.0, 0.0) + jnp.where(meta[1] == number, 1.0, 0.0)
    load = jnp.sum(mine, axis=1, keepdims=True)
    return jnp.sum(jnp.where(load > float(light), 1.0, 0.0), axis=0, keepdims=True)


NT = (((1,), (1,)), ((), ()))
TN = (((0,), (0,)), ((), ()))


class Copies:
    def __init__(self, sems):
        self.sems, self.started = sems, []

    def start(self, src, dst):
        copy = pltpu.make_async_copy(src, dst, self.sems.at[len(self.started)])
        copy.start()
        self.started.append(copy)
        return copy


def blocks_of(size):
    block = min(256, size)
    return block, size // block


def forward_kernel(count, cap, light, split, shadow, load_in, own, sib, *refs):
    weights, load_out, outs, scratch = refs[0:6], refs[6], refs[7 : 11 + split], refs[11 + split :]
    vg, vu, vd, rows_in, rows_out, meta, x_s, g_s, p_s, place_s, sems = scratch
    rows, hidden = rows_in.shape[0] // 2, vg.shape[2]
    copies = Copies(sems)
    loads = []
    for core, src in enumerate((own, sib)):
        at = pl.ds(core * rows, rows)
        loads.append(copies.start(src.at[pl.ds(2 * rows, META), pl.ds(0, rows)], meta.at[:, at]))
        loads.append(copies.start(src.at[pl.ds(0, rows)], rows_in.at[at]))
        loads.append(copies.start(src.at[pl.ds(rows, rows)], rows_out.at[at]))
    ready = {}
    for s in range(3):
        if s == 1:
            for load in loads:
                load.wait()
        for i, (src, extra, dst) in enumerate(zip(weights[0:3], weights[3:6], (vg, vu, vd))):
            ready[3 * s + i] = copies.start(src.at[s] if s < 2 else extra.at[0], dst.at[s])
    routes = routing(meta[...])
    load_out[...] = load_in[...] + heavy_loads(routes, count, light)
    codes, gate = row_codes(routes, copy_numbers(shadow, count))
    place, x_s[...], g_s[...] = gather_rows(
        codes, gate, range(5), cap, rows_in[...], rows_out[...]
    )
    place_s[...] = place[0 : 3 * cap]
    stores = [copies.start(a, b) for a, b in zip((x_s, g_s, place_s), (outs[0], outs[1], outs[2]))]
    for s in range(3):
        at = slice(s * cap, (s + 1) * cap)
        inputs, grads = x_s[at, :], g_s[at, :]
        ready[3 * s].wait()
        p_s[at, 0:hidden] = jnp.dot(
            inputs, vg[s], preferred_element_type=jnp.float32
        ).astype(jnp.bfloat16)
        ready[3 * s + 1].wait()
        p_s[at, hidden : 2 * hidden] = jnp.dot(
            inputs, vu[s], preferred_element_type=jnp.float32
        ).astype(jnp.bfloat16)
        ready[3 * s + 2].wait()
        p_s[at, 2 * hidden :] = lax.dot_general(
            grads, vd[s], NT, preferred_element_type=jnp.float32
        ).astype(jnp.bfloat16)
        of = pl.ds(s * cap, cap)
        stores.append(copies.start(p_s.at[of], outs[4] if split and s == 2 else outs[3].at[of]))
    for store in stores:
        store.wait()


def choose_kernel(moves, which, load, other, last):
    heavy = jnp.max(load[...] + other[...]) > 0.0
    last[0] = which[0] + jnp.where(heavy, moves, 0)


def activation(partial, hidden):
    full = partial[0].astype(jnp.float32)
    for other in partial[1:]:
        full = full + other.astype(jnp.float32)
    gate, up, down = full[:, 0:hidden], full[:, hidden : 2 * hidden], full[:, 2 * hidden :]
    sig = 1.0 / (1.0 + jnp.exp(-gate))
    swish = gate * sig
    return (
        (down * up * sig * (1.0 + gate * (1.0 - sig))).astype(jnp.bfloat16),
        (down * swish).astype(jnp.bfloat16),
        (swish * up).astype(jnp.bfloat16),
    )


def token_grads(grad_gate, grad_up, place, gate_weight, up_weight):
    route = lax.dot_general(grad_gate, gate_weight, NT, preferred_element_type=jnp.float32)
    route = route + lax.dot_general(grad_up, up_weight, NT, preferred_element_type=jnp.float32)
    return lax.dot_general(
        place, route.astype(jnp.bfloat16), TN, preferred_element_type=jnp.float32
    )


def backward_kernel(parts, split, cap, light, *refs):
    pieces = 2 if split else 1
    partial = [refs[pieces * i : pieces * (i + 1)] for i in range(parts)]
    refs = refs[pieces * parts :]
    place_in, weights, refs = refs[0], refs[1:5], refs[5:]
    kinds = 2 if light < cap else 1
    a_out, shadow_outs, own_out, sib_out = refs[0], refs[1 : 1 + kinds], *refs[1 + kinds : 3 + kinds]
    vg, vu, part_s, place_s, a_s, total, own_s, sib_s, sems = refs[3 + kinds :]
    hidden, rows = vg.shape[2], own_s.shape[0]
    copies = Copies(sems)
    loads, ready, stores = [], [], []
    for s in range(3):
        of = pl.ds(s * cap, cap)
        loads.append([])
        for i, p in enumerate(partial):
            src = p[1] if split and s == 2 else p[0].at[of]
            loads[s].append(copies.start(src, part_s.at[i, of]))
        loads[s].append(copies.start(place_in.at[of], place_s.at[of]))
        for src, extra, dst in zip(weights[0:2], weights[2:4], (vg, vu)):
            ready.append(copies.start(src.at[s] if s < 2 else extra.at[0], dst.at[s]))
    for s in range(3):
        at, of = slice(s * cap, (s + 1) * cap), pl.ds(s * cap, cap)
        for load in loads[s]:
            load.wait()
        grads = activation([part_s[i, at, :] for i in range(parts)], hidden)
        for i in range(3):
            a_s[at, i * hidden : (i + 1) * hidden] = grads[i]
        if s < 2:
            stores.append(copies.start(a_s.at[of], a_out.at[of]))
        else:
            first = 2 * cap
            for kind, size in enumerate((light, cap - light)[0:kinds]):
                stores.append(copies.start(a_s.at[pl.ds(first, size)], shadow_outs[kind]))
                first += size
        ready[2 * s].wait()
        ready[2 * s + 1].wait()
        part = token_grads(grads[0], grads[1], place_s[at, :], vg[s], vu[s])
        if s == 0:
            total[...] = part
        elif s == 1:
            total[...] += part
        else:
            part = total[...] + part
            own_s[...] = part[0:rows].astype(jnp.bfloat16)
            sib_s[...] = part[rows : 2 * rows].astype(jnp.bfloat16)
            stores.append(copies.start(own_s, own_out))
            stores.append(copies.start(sib_s, sib_out))
    for store in stores:
        store.wait()


def weights_kernel(count, cap, light, pieces, heavy_from, shadow, which, *refs):
    arrays = sum(n for _, n in pieces)
    owned, whole, near = cap * count, cap * count, light * count
    xs, gs, acts = refs[0:count], refs[count : 2 * count], refs[2 * count : 3 * count]
    refs = refs[3 * count :]
    shadow_acts = refs[0:arrays]
    og, ou, od, x_all, g_all, a_all, og_s, ou_s, od_s, sems, slot_sems = refs[arrays:]
    width, hidden = og_s.shape[1], og_s.shape[2]

    def owned_copies(e):
        copies = []
        for i in range(count):
            to, of = pl.ds(i * cap, cap), pl.ds(pl.multiple_of(e * cap, 16), cap)
            for j, (srcs, dst) in enumerate(((xs, x_all), (gs, g_all), (acts, a_all))):
                sem = sems.at[e * 3 * count + 3 * i + j]
                copies.append(pltpu.make_async_copy(srcs[i].at[of], dst.at[e, to], sem))
        return copies

    heavy = which[0] >= heavy_from
    held = held_for(shadow, count)
    last = jnp.where(held[0][1] == 0, 0, 1)
    for e in (1 - last, last):
        for copy in owned_copies(e):
            copy.start()
    together = held[0][1] == held[1][1]
    after_first = jnp.where(together, jnp.where(heavy, whole, near), 0)

    def slot_copies(slot, act):
        e = jnp.maximum(held[slot][1], 0)
        start = owned if slot == 0 else owned + after_first
        z, found = position()[0], held[slot][1] >= 0
        rest, first = cap - light, (3 + slot) * cap
        plans = []
        for k in range(count):
            part = held[slot][0] ^ z ^ k
            for src, dst in ((xs[k], x_all), (gs[k], g_all)):
                plans.append((found, src.at[pl.ds(first, light)], dst, part * light, light))
                if rest:
                    src = src.at[pl.ds(first + light, rest)]
                    plans.append((found & heavy, src, dst, near + part * rest, rest))
        at, i = 0, 0
        for size, number in pieces:
            for n in range(number):
                when = found if at < near else found & heavy
                if number == count - 1:
                    when = when & ((held[slot][0] ^ z) == n + 1)
                if number == count - 1 or n == slot:
                    plans.append((when, shadow_acts[i], a_all, at, size))
                i += 1
            at += size
        for number, (when, src, dst, at, size) in enumerate(plans):
            to = pl.ds(pl.multiple_of(start + at, 16), size)
            sem = slot_sems.at[slot, number]

            @pl.when(when)
            def _(src=src, dst=dst, to=to, sem=sem):
                act(pltpu.make_async_copy(src, dst.at[e, to], sem))

    def for_slots(act):
        for slot in range(2):
            slot_copies(slot, act)

    for_slots(lambda copy: copy.start())
    f_block, f_blocks = blocks_of(width)
    h_block, h_blocks = blocks_of(hidden)

    def results(e):
        return [
            pltpu.make_async_copy(src.at[e], dst.at[e], sems.at[e * 3 * count + i])
            for i, (src, dst) in enumerate(((og_s, og), (ou_s, ou), (od_s, od)))
        ]

    def products(e, k):
        for j in range(f_blocks):
            of = slice(j * f_block, (j + 1) * f_block)
            both = lax.dot_general(
                x_all[e, 0:k, of],
                a_all[e, 0:k, 0 : 2 * hidden],
                TN,
                preferred_element_type=jnp.float32,
            ).astype(jnp.bfloat16)
            og_s[e, of, :] = both[:, 0:hidden]
            ou_s[e, of, :] = both[:, hidden:]
        for copy in results(e)[0:2]:
            copy.start()
        for j in range(h_blocks):
            of = slice(j * h_block, (j + 1) * h_block)
            from_ = slice(2 * hidden + j * h_block, 2 * hidden + (j + 1) * h_block)
            od_s[e, of, :] = lax.dot_general(
                a_all[e, 0:k, from_], g_all[e, 0:k, :], TN, preferred_element_type=jnp.float32
            ).astype(jnp.bfloat16)

    def turn(n, _):
        e = jnp.where(n == 0, 1 - last, last)
        for copy in owned_copies(e):
            copy.wait()

        @pl.when(n == jnp.where(together, 1, 0))
        def _():
            for_slots(lambda copy: copy.wait())

        first = jnp.where(held[0][1] == e, 1, 0)
        slots = first + jnp.where(held[1][1] == e, 1, 0)

        @pl.when(slots == 0)
        def _():
            products(e, owned)

        for number in (1, 2):
            if near < whole:

                @pl.when((slots == number) & ~heavy)
                def _(number=number):
                    products(e, owned + number * near)

            @pl.when((slots == number) & heavy)
            def _(number=number):
                products(e, owned + number * whole)

        results(e)[2].start()
        return 0

    lax.fori_loop(0, 2, turn, 0)
    for e in range(2):
        for copy in results(e):
            copy.wait()


def shadow_moves():
    moves = {}
    for code in range(256):
        owners = [(code >> (2 * j)) & 3 for j in range(4)]
        if any(owners[j] == j for j in range(4)):
            continue
        if sorted(owners.count(i) for i in range(4)) != [0, 0, 2, 2]:
            continue
        apart = sorted({j ^ owners[j] for j in range(4)})
        if 1 in apart:
            perms = [[(j, j ^ d) for j in range(4)] for d in apart]
        else:
            perms = [[(j, o) for j, o in enumerate(owners) if j ^ o == d] for d in apart]
        key = tuple(tuple(p) for p in perms)
        moves.setdefault(key, []).append(owners)
    return list(moves.items())


def after(value, *others):
    return lax.optimization_barrier((value, *others))[0]


def on_device(
    tokens,
    out_grad,
    expert_ids,
    gate_weights,
    shadow_expert,
    w_gate,
    w_up,
    w_down,
    copy_gate,
    copy_up,
    copy_down,
):
    bf16 = jnp.bfloat16
    rows, width = tokens.shape
    hidden = w_gate.shape[2]
    count, dp_count = lax.axis_size("expert"), lax.axis_size("dp")
    cap = -(-2 * max(2, 3 * rows // (2 * count)) // 16) * 16
    light = -(-2 * cap // 3 // 16) * 16
    swap = [(0, 1), (1, 0)]
    shape = jax.ShapeDtypeStruct

    def to_index(x, k):
        return lax.ppermute(x, "expert", [(i, i ^ k) for i in range(count)])

    def swapped(x):
        return lax.ppermute(x, "inner", swap)

    def forward(load, own, sib, split=0):
        outs = (
            shape((8, 128), jnp.float32),
            shape((5 * cap, width), bf16),
            shape((5 * cap, width), bf16),
            shape((3 * cap, 2 * rows), bf16),
            *[shape((n * cap, 3 * hidden), bf16) for n in ((2, 1) if split else (3,))],
        )
        return call(
            functools.partial(forward_kernel, count, cap, light, split),
            outs,
            [SCALARS, WHOLE] + [REMAIN] * 8,
            (WHOLE,) + (REMAIN,) * (len(outs) - 1),
            [
                pltpu.VMEM((3, width, hidden), bf16),
                pltpu.VMEM((3, width, hidden), bf16),
                pltpu.VMEM((3, hidden, width), bf16),
                pltpu.VMEM((2 * rows, width), bf16),
                pltpu.VMEM((2 * rows, width), bf16),
                pltpu.VMEM((META, 2 * rows), bf16),
                pltpu.VMEM((5 * cap, width), bf16),
                pltpu.VMEM((5 * cap, width), bf16),
                pltpu.VMEM((3 * cap, 3 * hidden), bf16),
                pltpu.VMEM((3 * cap, 2 * rows), bf16),
                pltpu.SemaphoreType.DMA((21,)),
            ],
        )(shadow_expert, load, own, sib, w_gate, w_up, w_down, copy_gate, copy_up, copy_down)

    def exchange(partial):
        if dp_count == 2:
            return [partial, lax.ppermute(partial, "dp", swap)]
        return [lax.psum(partial, "dp")]

    def backward(partials, place):
        parts, split = len(partials), len(partials[0]) - 1
        outs = [shape((2 * cap, 3 * hidden), bf16), shape((light, 3 * hidden), bf16)]
        if light < cap:
            outs.append(shape((cap - light, 3 * hidden), bf16))
        outs += [shape((rows, width), bf16)] * 2
        return call(
            functools.partial(backward_kernel, parts, split, cap, light),
            outs,
            [REMAIN] * ((1 + split) * parts + 5),
            [REMAIN] * len(outs),
            [
                pltpu.VMEM((3, width, hidden), bf16),
                pltpu.VMEM((3, width, hidden), bf16),
                pltpu.VMEM((parts, 3 * cap, 3 * hidden), bf16),
                pltpu.VMEM((3 * cap, 2 * rows), bf16),
                pltpu.VMEM((3 * cap, 3 * hidden), bf16),
                pltpu.VMEM((2 * rows, width), jnp.float32),
                pltpu.VMEM((rows, width), bf16),
                pltpu.VMEM((rows, width), bf16),
                pltpu.SemaphoreType.DMA((17 + 3 * parts,)),
            ],
        )(*[p for x in partials for p in x], place, w_gate, w_up, copy_gate, copy_up)

    def give_back(dx_own, dx_sib, k):
        both = dx_own.astype(jnp.float32) + swapped(dx_sib).astype(jnp.float32)
        return to_index(both.astype(bf16), k) if k else both

    def add_up(returned):
        total = returned[0]
        for x in returned[1:]:
            total = total + x.astype(jnp.float32)
        return total.astype(bf16)

    def weight_grads(kept, pieces, which, heavy_from):
        layout = [(p[0].shape[0], len(p)) for p in pieces]
        outs = (
            shape((2, width, hidden), bf16),
            shape((2, width, hidden), bf16),
            shape((2, hidden, width), bf16),
        )
        most = cap * count * 3
        arrays = [
            *[k[0] for k in kept],
            *[k[1] for k in kept],
            *[k[2] for k in kept],
            *[x for p in pieces for x in p],
        ]
        return call(
            functools.partial(weights_kernel, count, cap, light, layout, heavy_from),
            outs,
            [SCALARS, SCALARS] + [REMAIN] * len(arrays),
            (REMAIN,) * 3,
            [
                pltpu.VMEM((2, most, width), bf16),
                pltpu.VMEM((2, most, width), bf16),
                pltpu.VMEM((2, most, 3 * hidden), bf16),
                *[pltpu.VMEM(o.shape, bf16) for o in outs],
                pltpu.SemaphoreType.DMA((6 * count,)),
                pltpu.SemaphoreType.DMA((2, 4 * count + sum(n for _, n in layout))),
            ],
        )(shadow_expert, which, *arrays)

    own, which = call(
        functools.partial(pack_kernel, count),
        (shape((2 * rows + META, width), bf16), shape((1,), jnp.int32)),
        [SCALARS] + [WHOLE] * 4,
        (WHOLE, SCALARS),
        [],
    )(shadow_expert, tokens, out_grad, expert_ids.T, gate_weights.T)
    load = jnp.zeros((8, 128), jnp.float32)
    if count != 4:
        kept, returned, shadow_acts = [], [], []
        for k in range(count):
            here = to_index(own, k) if k else own
            sib = swapped(here)
            load, inputs, grads, place, partial = forward(load, here, sib)
            acts, *shadow_part, dx_own, dx_sib = backward([[p] for p in exchange(partial)], place)
            returned.append(give_back(dx_own, dx_sib, k))
            kept.append((inputs, grads, acts))
            shadow_acts += shadow_part
        whole = lax.all_gather(jnp.concatenate(shadow_acts, axis=0), "expert")
        z = lax.axis_index("expert")
        apart = jnp.arange(count, dtype=jnp.int32) ^ z
        held = shadow_expert // 2 == z
        near = jnp.min(jnp.where(held, apart, count - 1))
        far = jnp.max(jnp.where(held, apart, 0))
        near = lax.dynamic_index_in_dim(whole, z ^ near, 0, keepdims=False)
        far = lax.dynamic_index_in_dim(whole, z ^ far, 0, keepdims=False)
        pieces = [[near, far]]
        return (add_up(returned), *weight_grads(kept, pieces, which, 0))

    moves = [perms for perms, _ in shadow_moves()]

    def everywhere(x):
        two = to_index(x, 2)
        return [to_index(x, 1), two, to_index(two, 1)]

    here1 = to_index(own, 1)
    sib0 = swapped(own)
    load, x0, g0, place0, p0, q0 = forward(load, own, sib0, 1)
    t0 = lax.ppermute(q0, "dp", swap)
    r0 = lax.ppermute(p0, "dp", swap)
    here2 = to_index(after(own, q0), 2)
    sib1 = swapped(after(here1, t0))
    load, x1, g1, place1, p1, q1 = forward(load, here1, sib1, 1)
    p1, q1 = after((p1, q1), r0)
    t1 = lax.ppermute(q1, "dp", swap)
    r1 = lax.ppermute(p1, "dp", swap)
    here3 = to_index(here2, 1)
    a0, near0, far0, dx_own0, dx_sib0 = backward([[p0, q0], [after(r0, p1), t0]], place0)
    sib2 = swapped(after(here2, a0, t1))
    moved0 = everywhere(near0)
    ret0 = give_back(dx_own0, dx_sib0, 0)
    load, x2, g2, place2, p2, q2 = forward(load, here2, sib2, 1)
    p2, q2 = after((p2, q2), r1)
    t2 = lax.ppermute(q2, "dp", swap)
    r2 = lax.ppermute(p2, "dp", swap)
    a1, near1, far1, dx_own1, dx_sib1 = backward(
        [[p1, q1], [after(r1, p2), t1]], place1
    )
    sib3 = swapped(after(here3, a1, t2, moved0[0], moved0[1]))
    moved1 = everywhere(near1)
    ret1 = give_back(dx_own1, dx_sib1, 1)
    load, x3, g3, place3, p3 = forward(load, here3, sib3)
    p3 = after(p3, r2)
    r3 = lax.ppermute(p3, "dp", swap)
    last = call(
        functools.partial(choose_kernel, len(moves)),
        shape((1,), jnp.int32),
        [SCALARS, WHOLE, WHOLE],
        SCALARS,
        [],
    )(which, load, lax.ppermute(load, "groups", swap))
    a2, near2, far2, dx_own2, dx_sib2 = backward(
        [[p2, q2], [after(r2, p3, moved0[2], moved1[0], moved1[1]), t2]], place2
    )
    ret2 = give_back(dx_own2, dx_sib2, 2)
    r3 = after(r3, last, ret1, ret2, moved1[2])
    a3, near3, far3, dx_own3, dx_sib3 = backward([[p3], [r3]], place3)
    near23 = jnp.concatenate([near2, near3], axis=0)

    rest = shape((count * (cap - light), 3 * hidden), bf16)

    def light_branch(perms, x, *more):
        unused = call(lambda *refs: None, (rest, rest), [], (REMAIN, REMAIN), [])()
        return [[lax.ppermute(x, "expert", p), u] for p, u in zip(perms, unused)]

    def heavy_branch(perms, x, *more):
        more = jnp.concatenate(more, axis=0)
        return [[lax.ppermute(y, "expert", p) for y in (x, more)] for p in perms]

    moved23 = lax.switch(
        last[0],
        [functools.partial(f, m) for f in (light_branch, heavy_branch) for m in moves],
        near23,
        far0,
        far1,
        far2,
        far3,
    )
    ret3 = give_back(dx_own3, dx_sib3, 3)
    pieces = [moved0, moved1, [m[0] for m in moved23], [m[1] for m in moved23]]
    kept = [(x0, g0, a0), (x1, g1, a1), (x2, g2, a2), (x3, g3, a3)]
    grads = weight_grads(kept, pieces, last, len(moves))
    return (add_up([ret0, ret1, ret2, ret3]), *grads)


def solution(mesh):
    return jax.shard_map(
        on_device,
        mesh=mesh,
        in_specs=(
            P(("groups", "expert", "inner"), "dp"),
            P(("groups", "expert", "inner"), "dp"),
            P(("groups", "expert", "inner"), None),
            P(("groups", "expert", "inner"), None),
            P(),
            P("expert", "dp", "inner"),
            P("expert", "dp", "inner"),
            P("expert", "inner", "dp"),
            P("expert", "dp", "inner"),
            P("expert", "dp", "inner"),
            P("expert", "inner", "dp"),
        ),
        out_specs=(
            P(("groups", "expert", "inner"), "dp"),
            P(("groups", "expert"), "dp", "inner"),
            P(("groups", "expert"), "dp", "inner"),
            P(("groups", "expert"), "inner", "dp"),
        ),
        check_vma=False,
    )
```

```python
import functools

import jax
import jax.numpy as jnp
from jax import lax
from jax.experimental import pallas as pl
from jax.experimental.pallas import tpu as pltpu
from jax.sharding import PartitionSpec as P

META = 16


def call(body, out_shape, in_specs, out_specs, scratch, **kw):
    return pl.pallas_call(
        body,
        out_shape=out_shape,
        in_specs=in_specs,
        out_specs=out_specs,
        scratch_shapes=scratch,
        compiler_params=pltpu.CompilerParams(vmem_limit_bytes=57 * 1024 * 1024),
        **kw,
    )


WHOLE = pl.BlockSpec(memory_space=pltpu.VMEM)
SCALARS = pl.BlockSpec(memory_space=pltpu.SMEM)
REMAIN = pl.BlockSpec(memory_space=pl.ANY)


def position():
    return lax.axis_index("expert"), lax.axis_index("inner")


def pack_kernel(shadow_count, shadow, tok_ref, grad_ref, ids_ref, gate_ref, out_ref, which_ref):
    rows = tok_ref.shape[0]
    out_ref[0:rows, :] = tok_ref[...]
    out_ref[rows : 2 * rows, :] = grad_ref[...]
    z, core = position()
    ids, gates = ids_ref[...].astype(jnp.float32), gate_ref[...]
    choice = lax.broadcasted_iota(jnp.int32, ids.shape, 0)
    place = (2 * z + core) * rows + lax.broadcasted_iota(jnp.int32, ids.shape, 1) + choice
    place = place.astype(jnp.float32)
    entry = [shadow[j] for j in range(shadow_count)]
    named = [ids == e.astype(jnp.float32) for e in entry]
    copies = jnp.ones(ids.shape, jnp.float32)
    for hit in named:
        copies = copies + jnp.where(hit, 1.0, 0.0)
    halves = place - 2.0 * jnp.floor((place + 0.5) * 0.5)
    thirds = place - 3.0 * jnp.floor((place + 0.5) * (1.0 / 3.0))
    chosen = jnp.where(copies == 2.0, halves, jnp.where(copies == 3.0, thirds, 0.0))
    serving = ids
    for j in range(shadow_count):
        before = jnp.int32(0)
        for i in range(j):
            before = before + jnp.where(entry[i] == entry[j], 1, 0)
        take = named[j] & (chosen == (before + 1).astype(jnp.float32))
        serving = jnp.where(take, float(2 * shadow_count + j), serving)
    high = gates.astype(jnp.bfloat16)
    rest = gates - high.astype(jnp.float32)
    middle = rest.astype(jnp.bfloat16)
    low = (rest - middle.astype(jnp.float32)).astype(jnp.bfloat16)
    block = jnp.concatenate(
        [
            serving,
            high.astype(jnp.float32),
            middle.astype(jnp.float32),
            low.astype(jnp.float32),
            jnp.zeros((META - 8, rows), jnp.float32),
        ],
        axis=0,
    )
    out_ref[2 * rows : 2 * rows + META, :] = jnp.zeros((META, tok_ref.shape[1]), jnp.bfloat16)
    out_ref[2 * rows : 2 * rows + META, 0:rows] = block.astype(jnp.bfloat16)
    which = jnp.int32(0)
    if shadow_count == 4:
        for i, (_, placements) in enumerate(shadow_moves()):
            for owners in placements:
                same = jnp.bool_(True)
                for j in range(4):
                    same = same & (entry[j] // 2 == owners[j])
                which = jnp.where(same, i, which)
    which_ref[0] = which


def routing(meta):
    meta = meta.astype(jnp.float32)
    return meta[0:1], meta[1:2], meta[2:3] + meta[4:5] + meta[6:7], meta[3:4] + meta[5:6] + meta[7:8]


def row_codes(meta, numbers):
    first, second, gate_a, gate_b = meta
    tokens = first.shape[1]
    hit_a, hit_b = first == numbers, second == numbers
    hit = jnp.where(hit_a | hit_b, 1.0, 0.0)
    gate = jnp.where(hit_a, gate_a, 0.0) + jnp.where(hit_b, gate_b, 0.0)
    earlier = lax.broadcasted_iota(jnp.int32, (tokens, tokens), 0) < lax.broadcasted_iota(
        jnp.int32, (tokens, tokens), 1
    )
    rank = jnp.dot(
        hit.astype(jnp.bfloat16),
        jnp.where(earlier, 1.0, 0.0).astype(jnp.bfloat16),
        preferred_element_type=jnp.float32,
    )
    return jnp.where(hit > 0.0, rank, -1.0), gate


def gather_rows(codes, gate, wanted, cap, tok, grad):
    tokens = codes.shape[1]
    row = lax.broadcasted_iota(jnp.int32, (cap, tokens), 0).astype(jnp.float32)
    places, gates = [], []
    for s in wanted:
        place = row == codes[s : s + 1, :]
        gates.append(
            jnp.sum(jnp.where(place, gate[s : s + 1, :], 0.0), axis=1, keepdims=True)
        )
        places.append(jnp.where(place, 1.0, 0.0).astype(jnp.bfloat16))
    place = places[0] if len(places) == 1 else jnp.concatenate(places, axis=0)
    row_gate = gates[0] if len(gates) == 1 else jnp.concatenate(gates, axis=0)
    inputs = jnp.dot(place, tok, preferred_element_type=jnp.float32).astype(jnp.bfloat16)
    grads = jnp.dot(place, grad, preferred_element_type=jnp.float32)
    return place, inputs, (grads * row_gate).astype(jnp.bfloat16)


def held_for(shadow, count):
    z = position()[0]
    near, far = jnp.int32(0), jnp.int32(0)
    for k in range(1, count):
        mine = shadow[z ^ k] // 2 == z
        near = jnp.where(mine & (near == 0), k, near)
        far = jnp.where(mine, k, far)
    found = near > 0
    return tuple(
        (z ^ k, jnp.where(found, shadow[z ^ k] - 2 * z, -1)) for k in (near, far)
    )


def copy_numbers(shadow, count):
    z = position()[0]
    slot = lax.broadcasted_iota(jnp.int32, (8, 1), 0)
    number = jnp.where(slot < 2, 2 * z + slot, jnp.where(slot == 2, 2 * count + z, -1))
    for i, (holder, of) in enumerate(held_for(shadow, count)):
        number = jnp.where(slot == 3 + i, jnp.where(of >= 0, 2 * count + holder, -1), number)
    return number.astype(jnp.float32)


def heavy_loads(meta, count, light):
    holder = lax.broadcasted_iota(jnp.int32, (-(-count // 8) * 8, 1), 0)
    number = jnp.where(holder < count, 2 * count + holder, -1).astype(jnp.float32)
    mine = jnp.where(meta[0] == number, 1.0, 0.0) + jnp.where(meta[1] == number, 1.0, 0.0)
    load = jnp.sum(mine, axis=1, keepdims=True)
    return jnp.sum(jnp.where(load > float(light), 1.0, 0.0), axis=0, keepdims=True)


NT = (((1,), (1,)), ((), ()))
TN = (((0,), (0,)), ((), ()))


class Copies:
    def __init__(self, sems):
        self.sems, self.started = sems, []

    def start(self, src, dst):
        copy = pltpu.make_async_copy(src, dst, self.sems.at[len(self.started)])
        copy.start()
        self.started.append(copy)
        return copy


def blocks_of(size):
    block = min(256, size)
    return block, size // block


def forward_kernel(count, cap, light, split, shadow, load_in, own, sib, *refs):
    weights, load_out, outs, scratch = refs[0:6], refs[6], refs[7 : 11 + split], refs[11 + split :]
    vg, vu, vd, rows_in, rows_out, meta, x_s, g_s, p_s, place_s, sems = scratch
    rows, hidden = rows_in.shape[0] // 2, vg.shape[2]
    copies = Copies(sems)
    loads = []
    for core, src in enumerate((own, sib)):
        at = pl.ds(core * rows, rows)
        loads.append(copies.start(src.at[pl.ds(2 * rows, META), pl.ds(0, rows)], meta.at[:, at]))
        loads.append(copies.start(src.at[pl.ds(0, rows)], rows_in.at[at]))
        loads.append(copies.start(src.at[pl.ds(rows, rows)], rows_out.at[at]))
    ready = {}
    for s in range(3):
        if s == 1:
            for load in loads:
                load.wait()
        for i, (src, extra, dst) in enumerate(zip(weights[0:3], weights[3:6], (vg, vu, vd))):
            ready[3 * s + i] = copies.start(src.at[s] if s < 2 else extra.at[0], dst.at[s])
    routes = routing(meta[...])
    load_out[...] = load_in[...] + heavy_loads(routes, count, light)
    codes, gate = row_codes(routes, copy_numbers(shadow, count))
    place, x_s[...], g_s[...] = gather_rows(
        codes, gate, range(5), cap, rows_in[...], rows_out[...]
    )
    place_s[...] = place[0 : 3 * cap]
    stores = [copies.start(a, b) for a, b in zip((x_s, g_s, place_s), (outs[0], outs[1], outs[2]))]
    for s in range(3):
        at = slice(s * cap, (s + 1) * cap)
        inputs, grads = x_s[at, :], g_s[at, :]
        ready[3 * s].wait()
        p_s[at, 0:hidden] = jnp.dot(
            inputs, vg[s], preferred_element_type=jnp.float32
        ).astype(jnp.bfloat16)
        ready[3 * s + 1].wait()
        p_s[at, hidden : 2 * hidden] = jnp.dot(
            inputs, vu[s], preferred_element_type=jnp.float32
        ).astype(jnp.bfloat16)
        ready[3 * s + 2].wait()
        p_s[at, 2 * hidden :] = lax.dot_general(
            grads, vd[s], NT, preferred_element_type=jnp.float32
        ).astype(jnp.bfloat16)
        of = pl.ds(s * cap, cap)
        stores.append(copies.start(p_s.at[of], outs[4] if split and s == 2 else outs[3].at[of]))
    for store in stores:
        store.wait()


def choose_kernel(moves, which, load, other, last):
    heavy = jnp.max(load[...] + other[...]) > 0.0
    last[0] = which[0] + jnp.where(heavy, moves, 0)


def activation(partial, hidden):
    full = partial[0].astype(jnp.float32)
    for other in partial[1:]:
        full = full + other.astype(jnp.float32)
    gate, up, down = full[:, 0:hidden], full[:, hidden : 2 * hidden], full[:, 2 * hidden :]
    sig = 1.0 / (1.0 + jnp.exp(-gate))
    swish = gate * sig
    return (
        (down * up * sig * (1.0 + gate * (1.0 - sig))).astype(jnp.bfloat16),
        (down * swish).astype(jnp.bfloat16),
        (swish * up).astype(jnp.bfloat16),
    )


def token_grads(grad_gate, grad_up, place, gate_weight, up_weight):
    route = lax.dot_general(grad_gate, gate_weight, NT, preferred_element_type=jnp.float32)
    route = route + lax.dot_general(grad_up, up_weight, NT, preferred_element_type=jnp.float32)
    return lax.dot_general(
        place, route.astype(jnp.bfloat16), TN, preferred_element_type=jnp.float32
    )


def backward_kernel(parts, split, cap, light, *refs):
    pieces = 2 if split else 1
    partial = [refs[pieces * i : pieces * (i + 1)] for i in range(parts)]
    refs = refs[pieces * parts :]
    place_in, weights, refs = refs[0], refs[1:5], refs[5:]
    kinds = 2 if light < cap else 1
    a_out, shadow_outs, own_out, sib_out = refs[0], refs[1 : 1 + kinds], *refs[1 + kinds : 3 + kinds]
    vg, vu, part_s, place_s, a_s, total, own_s, sib_s, sems = refs[3 + kinds :]
    hidden, rows = vg.shape[2], own_s.shape[0]
    copies = Copies(sems)
    loads, ready, stores = [], [], []
    for s in range(3):
        of = pl.ds(s * cap, cap)
        loads.append([])
        for i, p in enumerate(partial):
            src = p[1] if split and s == 2 else p[0].at[of]
            loads[s].append(copies.start(src, part_s.at[i, of]))
        loads[s].append(copies.start(place_in.at[of], place_s.at[of]))
        for src, extra, dst in zip(weights[0:2], weights[2:4], (vg, vu)):
            ready.append(copies.start(src.at[s] if s < 2 else extra.at[0], dst.at[s]))
    for s in range(3):
        at, of = slice(s * cap, (s + 1) * cap), pl.ds(s * cap, cap)
        for load in loads[s]:
            load.wait()
        grads = activation([part_s[i, at, :] for i in range(parts)], hidden)
        for i in range(3):
            a_s[at, i * hidden : (i + 1) * hidden] = grads[i]
        if s < 2:
            stores.append(copies.start(a_s.at[of], a_out.at[of]))
        else:
            first = 2 * cap
            for kind, size in enumerate((light, cap - light)[0:kinds]):
                stores.append(copies.start(a_s.at[pl.ds(first, size)], shadow_outs[kind]))
                first += size
        ready[2 * s].wait()
        ready[2 * s + 1].wait()
        part = token_grads(grads[0], grads[1], place_s[at, :], vg[s], vu[s])
        if s == 0:
            total[...] = part
        elif s == 1:
            total[...] += part
        else:
            part = total[...] + part
            own_s[...] = part[0:rows].astype(jnp.bfloat16)
            sib_s[...] = part[rows : 2 * rows].astype(jnp.bfloat16)
            stores.append(copies.start(own_s, own_out))
            stores.append(copies.start(sib_s, sib_out))
    for store in stores:
        store.wait()


def weights_kernel(count, cap, light, pieces, heavy_from, shadow, which, *refs):
    arrays = sum(n for _, n in pieces)
    owned, whole, near = cap * count, cap * count, light * count
    xs, gs, acts = refs[0:count], refs[count : 2 * count], refs[2 * count : 3 * count]
    refs = refs[3 * count :]
    shadow_acts = refs[0:arrays]
    og, ou, od, x_all, g_all, a_all, og_s, ou_s, od_s, sems, slot_sems = refs[arrays:]
    width, hidden = og_s.shape[1], og_s.shape[2]

    def owned_copies(e):
        copies = []
        for i in range(count):
            to, of = pl.ds(i * cap, cap), pl.ds(pl.multiple_of(e * cap, 16), cap)
            for j, (srcs, dst) in enumerate(((xs, x_all), (gs, g_all), (acts, a_all))):
                sem = sems.at[e * 3 * count + 3 * i + j]
                copies.append(pltpu.make_async_copy(srcs[i].at[of], dst.at[e, to], sem))
        return copies

    heavy = which[0] >= heavy_from
    held = held_for(shadow, count)
    last = jnp.where(held[0][1] == 0, 0, 1)
    for e in (1 - last, last):
        for copy in owned_copies(e):
            copy.start()
    together = held[0][1] == held[1][1]
    after_first = jnp.where(together, jnp.where(heavy, whole, near), 0)

    def slot_copies(slot, act):
        e = jnp.maximum(held[slot][1], 0)
        start = owned if slot == 0 else owned + after_first
        z, found = position()[0], held[slot][1] >= 0
        rest, first = cap - light, (3 + slot) * cap
        plans = []
        for k in range(count):
            part = held[slot][0] ^ z ^ k
            for src, dst in ((xs[k], x_all), (gs[k], g_all)):
                plans.append((found, src.at[pl.ds(first, light)], dst, part * light, light))
                if rest:
                    src = src.at[pl.ds(first + light, rest)]
                    plans.append((found & heavy, src, dst, near + part * rest, rest))
        at, i = 0, 0
        for size, number in pieces:
            for n in range(number):
                when = found if at < near else found & heavy
                if number == count - 1:
                    when = when & ((held[slot][0] ^ z) == n + 1)
                if number == count - 1 or n == slot:
                    plans.append((when, shadow_acts[i], a_all, at, size))
                i += 1
            at += size
        for number, (when, src, dst, at, size) in enumerate(plans):
            to = pl.ds(pl.multiple_of(start + at, 16), size)
            sem = slot_sems.at[slot, number]

            @pl.when(when)
            def _(src=src, dst=dst, to=to, sem=sem):
                act(pltpu.make_async_copy(src, dst.at[e, to], sem))

    def for_slots(act):
        for slot in range(2):
            slot_copies(slot, act)

    for_slots(lambda copy: copy.start())
    f_block, f_blocks = blocks_of(width)
    h_block, h_blocks = blocks_of(hidden)

    def results(e):
        return [
            pltpu.make_async_copy(src.at[e], dst.at[e], sems.at[e * 3 * count + i])
            for i, (src, dst) in enumerate(((og_s, og), (ou_s, ou), (od_s, od)))
        ]

    def products(e, k):
        for j in range(f_blocks):
            of = slice(j * f_block, (j + 1) * f_block)
            both = lax.dot_general(
                x_all[e, 0:k, of],
                a_all[e, 0:k, 0 : 2 * hidden],
                TN,
                preferred_element_type=jnp.float32,
            ).astype(jnp.bfloat16)
            og_s[e, of, :] = both[:, 0:hidden]
            ou_s[e, of, :] = both[:, hidden:]
        for copy in results(e)[0:2]:
            copy.start()
        for j in range(h_blocks):
            of = slice(j * h_block, (j + 1) * h_block)
            from_ = slice(2 * hidden + j * h_block, 2 * hidden + (j + 1) * h_block)
            od_s[e, of, :] = lax.dot_general(
                a_all[e, 0:k, from_], g_all[e, 0:k, :], TN, preferred_element_type=jnp.float32
            ).astype(jnp.bfloat16)

    def turn(n, _):
        e = jnp.where(n == 0, 1 - last, last)
        for copy in owned_copies(e):
            copy.wait()

        @pl.when(n == jnp.where(together, 1, 0))
        def _():
            for_slots(lambda copy: copy.wait())

        first = jnp.where(held[0][1] == e, 1, 0)
        slots = first + jnp.where(held[1][1] == e, 1, 0)

        @pl.when(slots == 0)
        def _():
            products(e, owned)

        for number in (1, 2):
            if near < whole:

                @pl.when((slots == number) & ~heavy)
                def _(number=number):
                    products(e, owned + number * near)

            @pl.when((slots == number) & heavy)
            def _(number=number):
                products(e, owned + number * whole)

        results(e)[2].start()
        return 0

    lax.fori_loop(0, 2, turn, 0)
    for e in range(2):
        for copy in results(e):
            copy.wait()


def shadow_moves():
    moves = {}
    for code in range(256):
        owners = [(code >> (2 * j)) & 3 for j in range(4)]
        if any(owners[j] == j for j in range(4)):
            continue
        if sorted(owners.count(i) for i in range(4)) != [0, 0, 2, 2]:
            continue
        apart = sorted({j ^ owners[j] for j in range(4)})
        if 1 in apart:
            perms = [[(j, j ^ d) for j in range(4)] for d in apart]
        else:
            perms = [[(j, o) for j, o in enumerate(owners) if j ^ o == d] for d in apart]
        key = tuple(tuple(p) for p in perms)
        moves.setdefault(key, []).append(owners)
    return list(moves.items())


def after(value, *others):
    return lax.optimization_barrier((value, *others))[0]


def on_device(
    tokens,
    out_grad,
    expert_ids,
    gate_weights,
    shadow_expert,
    w_gate,
    w_up,
    w_down,
    copy_gate,
    copy_up,
    copy_down,
):
    bf16 = jnp.bfloat16
    rows, width = tokens.shape
    hidden = w_gate.shape[2]
    count, dp_count = lax.axis_size("expert"), lax.axis_size("dp")
    cap = -(-2 * max(2, 3 * rows // (2 * count)) // 16) * 16
    light = -(-2 * cap // 3 // 16) * 16
    swap = [(0, 1), (1, 0)]
    shape = jax.ShapeDtypeStruct

    def to_index(x, k):
        return lax.ppermute(x, "expert", [(i, i ^ k) for i in range(count)])

    def swapped(x):
        return lax.ppermute(x, "inner", swap)

    def forward(load, own, sib, split=0):
        outs = (
            shape((8, 128), jnp.float32),
            shape((5 * cap, width), bf16),
            shape((5 * cap, width), bf16),
            shape((3 * cap, 2 * rows), bf16),
            *[shape((n * cap, 3 * hidden), bf16) for n in ((2, 1) if split else (3,))],
        )
        return call(
            functools.partial(forward_kernel, count, cap, light, split),
            outs,
            [SCALARS, WHOLE] + [REMAIN] * 8,
            (WHOLE,) + (REMAIN,) * (len(outs) - 1),
            [
                pltpu.VMEM((3, width, hidden), bf16),
                pltpu.VMEM((3, width, hidden), bf16),
                pltpu.VMEM((3, hidden, width), bf16),
                pltpu.VMEM((2 * rows, width), bf16),
                pltpu.VMEM((2 * rows, width), bf16),
                pltpu.VMEM((META, 2 * rows), bf16),
                pltpu.VMEM((5 * cap, width), bf16),
                pltpu.VMEM((5 * cap, width), bf16),
                pltpu.VMEM((3 * cap, 3 * hidden), bf16),
                pltpu.VMEM((3 * cap, 2 * rows), bf16),
                pltpu.SemaphoreType.DMA((21,)),
            ],
        )(shadow_expert, load, own, sib, w_gate, w_up, w_down, copy_gate, copy_up, copy_down)

    def exchange(partial):
        if dp_count == 2:
            return [partial, lax.ppermute(partial, "dp", swap)]
        return [lax.psum(partial, "dp")]

    def backward(partials, place):
        parts, split = len(partials), len(partials[0]) - 1
        outs = [shape((2 * cap, 3 * hidden), bf16), shape((light, 3 * hidden), bf16)]
        if light < cap:
            outs.append(shape((cap - light, 3 * hidden), bf16))
        outs += [shape((rows, width), bf16)] * 2
        return call(
            functools.partial(backward_kernel, parts, split, cap, light),
            outs,
            [REMAIN] * ((1 + split) * parts + 5),
            [REMAIN] * len(outs),
            [
                pltpu.VMEM((3, width, hidden), bf16),
                pltpu.VMEM((3, width, hidden), bf16),
                pltpu.VMEM((parts, 3 * cap, 3 * hidden), bf16),
                pltpu.VMEM((3 * cap, 2 * rows), bf16),
                pltpu.VMEM((3 * cap, 3 * hidden), bf16),
                pltpu.VMEM((2 * rows, width), jnp.float32),
                pltpu.VMEM((rows, width), bf16),
                pltpu.VMEM((rows, width), bf16),
                pltpu.SemaphoreType.DMA((17 + 3 * parts,)),
            ],
        )(*[p for x in partials for p in x], place, w_gate, w_up, copy_gate, copy_up)

    def give_back(dx_own, dx_sib, k):
        both = dx_own.astype(jnp.float32) + swapped(dx_sib).astype(jnp.float32)
        return to_index(both.astype(bf16), k) if k else both

    def add_up(returned):
        total = returned[0]
        for x in returned[1:]:
            total = total + x.astype(jnp.float32)
        return total.astype(bf16)

    def weight_grads(kept, pieces, which, heavy_from):
        layout = [(p[0].shape[0], len(p)) for p in pieces]
        outs = (
            shape((2, width, hidden), bf16),
            shape((2, width, hidden), bf16),
            shape((2, hidden, width), bf16),
        )
        most = cap * count * 3
        arrays = [
            *[k[0] for k in kept],
            *[k[1] for k in kept],
            *[k[2] for k in kept],
            *[x for p in pieces for x in p],
        ]
        return call(
            functools.partial(weights_kernel, count, cap, light, layout, heavy_from),
            outs,
            [SCALARS, SCALARS] + [REMAIN] * len(arrays),
            (REMAIN,) * 3,
            [
                pltpu.VMEM((2, most, width), bf16),
                pltpu.VMEM((2, most, width), bf16),
                pltpu.VMEM((2, most, 3 * hidden), bf16),
                *[pltpu.VMEM(o.shape, bf16) for o in outs],
                pltpu.SemaphoreType.DMA((6 * count,)),
                pltpu.SemaphoreType.DMA((2, 4 * count + sum(n for _, n in layout))),
            ],
        )(shadow_expert, which, *arrays)

    own, which = call(
        functools.partial(pack_kernel, count),
        (shape((2 * rows + META, width), bf16), shape((1,), jnp.int32)),
        [SCALARS] + [WHOLE] * 4,
        (WHOLE, SCALARS),
        [],
    )(shadow_expert, tokens, out_grad, expert_ids.T, gate_weights.T)
    load = jnp.zeros((8, 128), jnp.float32)
    if count != 4:
        kept, returned, shadow_acts = [], [], []
        for k in range(count):
            here = to_index(own, k) if k else own
            sib = swapped(here)
            load, inputs, grads, place, partial = forward(load, here, sib)
            acts, *shadow_part, dx_own, dx_sib = backward([[p] for p in exchange(partial)], place)
            returned.append(give_back(dx_own, dx_sib, k))
            kept.append((inputs, grads, acts))
            shadow_acts += shadow_part
        whole = lax.all_gather(jnp.concatenate(shadow_acts, axis=0), "expert")
        z = lax.axis_index("expert")
        apart = jnp.arange(count, dtype=jnp.int32) ^ z
        held = shadow_expert // 2 == z
        near = jnp.min(jnp.where(held, apart, count - 1))
        far = jnp.max(jnp.where(held, apart, 0))
        near = lax.dynamic_index_in_dim(whole, z ^ near, 0, keepdims=False)
        far = lax.dynamic_index_in_dim(whole, z ^ far, 0, keepdims=False)
        pieces = [[near, far]]
        return (add_up(returned), *weight_grads(kept, pieces, which, 0))

    moves = [perms for perms, _ in shadow_moves()]

    def everywhere(x):
        two = to_index(x, 2)
        return [to_index(x, 1), two, to_index(two, 1)]

    here1 = to_index(own, 1)
    sib0 = swapped(own)
    load, x0, g0, place0, p0, q0 = forward(load, own, sib0, 1)
    t0 = lax.ppermute(q0, "dp", swap)
    r0 = lax.ppermute(p0, "dp", swap)
    here2 = to_index(after(own, q0), 2)
    sib1 = swapped(after(here1, t0))
    load, x1, g1, place1, p1, q1 = forward(load, here1, sib1, 1)
    p1, q1 = after((p1, q1), r0)
    t1 = lax.ppermute(q1, "dp", swap)
    r1 = lax.ppermute(p1, "dp", swap)
    here3 = to_index(here2, 1)
    a0, near0, far0, dx_own0, dx_sib0 = backward([[p0, q0], [after(r0, p1), t0]], place0)
    sib2 = swapped(after(here2, a0, t1))
    moved0 = everywhere(near0)
    ret0 = give_back(dx_own0, dx_sib0, 0)
    load, x2, g2, place2, p2, q2 = forward(load, here2, sib2, 1)
    p2, q2 = after((p2, q2), r1)
    t2 = lax.ppermute(q2, "dp", swap)
    r2 = lax.ppermute(p2, "dp", swap)
    a1, near1, far1, dx_own1, dx_sib1 = backward(
        [[p1, q1], [after(r1, p2), t1]], place1
    )
    sib3 = swapped(after(here3, a1, t2, moved0[0], moved0[1]))
    moved1 = everywhere(near1)
    ret1 = give_back(dx_own1, dx_sib1, 1)
    load, x3, g3, place3, p3 = forward(load, here3, sib3)
    p3 = after(p3, r2)
    r3 = lax.ppermute(p3, "dp", swap)
    last = call(
        functools.partial(choose_kernel, len(moves)),
        shape((1,), jnp.int32),
        [SCALARS, WHOLE, WHOLE],
        SCALARS,
        [],
    )(which, load, lax.ppermute(load, "groups", swap))
    a2, near2, far2, dx_own2, dx_sib2 = backward(
        [[p2, q2], [after(r2, p3, moved0[2], moved1[0], moved1[1]), t2]], place2
    )
    ret2 = give_back(dx_own2, dx_sib2, 2)
    r3 = after(r3, last, ret1, ret2, moved1[2])
    a3, near3, far3, dx_own3, dx_sib3 = backward([[p3], [r3]], place3)
    near23 = jnp.concatenate([near2, near3], axis=0)

    rest = shape((count * (cap - light), 3 * hidden), bf16)

    def light_branch(perms, x, *more):
        unused = call(lambda *refs: None, (rest, rest), [], (REMAIN, REMAIN), [])()
        return [[lax.ppermute(x, "expert", p), u] for p, u in zip(perms, unused)]

    def heavy_branch(perms, x, *more):
        more = jnp.concatenate(more, axis=0)
        return [[lax.ppermute(y, "expert", p) for y in (x, more)] for p in perms]

    moved23 = lax.switch(
        last[0],
        [functools.partial(f, m) for f in (light_branch, heavy_branch) for m in moves],
        near23,
        far0,
        far1,
        far2,
        far3,
    )
    ret3 = give_back(dx_own3, dx_sib3, 3)
    pieces = [moved0, moved1, [m[0] for m in moved23], [m[1] for m in moved23]]
    kept = [(x0, g0, a0), (x1, g1, a1), (x2, g2, a2), (x3, g3, a3)]
    grads = weight_grads(kept, pieces, last, len(moves))
    return (add_up([ret0, ret1, ret2, ret3]), *grads)


def solution(mesh):
    return jax.shard_map(
        on_device,
        mesh=mesh,
        in_specs=(
            P(("groups", "expert", "inner"), "dp"),
            P(("groups", "expert", "inner"), "dp"),
            P(("groups", "expert", "inner"), None),
            P(("groups", "expert", "inner"), None),
            P(),
            P("expert", "dp", "inner"),
            P("expert", "dp", "inner"),
            P("expert", "inner", "dp"),
            P("expert", "dp", "inner"),
            P("expert", "dp", "inner"),
            P("expert", "inner", "dp"),
        ),
        out_specs=(
            P(("groups", "expert", "inner"), "dp"),
            P(("groups", "expert"), "dp", "inner"),
            P(("groups", "expert"), "dp", "inner"),
            P(("groups", "expert"), "inner", "dp"),
        ),
        check_vma=False,
    )
```
